128 devices in a mesh: ens: 8 (over x, core), map: 16 (over y, z).
Axes of the slice: x: 4, y: 4, z: 4, core: 2. Of those that a mesh axis runs over, the one named last changes fastest.
Arguments:
- ensemble_weather: bfloat16 [128, 16, 64, 1440], P('ens', None, 'map'), may hold values from -6 to 6
- conv_in: bfloat16 [128, 16, 3, 3], replicated, may hold values from -0.5 to 0.5
- bias_in: float32 [128], replicated, may hold values from -3 to 3
- conv_out: bfloat16 [16, 128, 3, 3], replicated, may hold values from -0.1875 to 0.1875
- bias_out: float32 [16], replicated, may hold values from -3 to 3
- observed_entry_index: int32 [4096], P('map'), may hold values from 0 to 92159
- obs_count: int32 [16], P('map'), may hold values from 128 to 256, as said below
- obs_value: float32 [4096], P('map'), may hold values from -8 to 8
- obs_sigma: float32 [4096], P('map'), may hold values from 0.5 to 2
Outputs:
- analysis: bfloat16 [128, 16, 64, 1440], P('ens', None, 'map')
- factor: float32 [128, 128], replicated
- mean_weights: float32 [128], replicated
The draws below stay inside these ranges and needn't reach their ends.
Inputs may be any that keep to these rules, and one draw needn't show every extreme that they name: `obs_count`: every draw has a tile with all 256 slots live.
All inputs are finite; a program needn't handle non-finite values.
Results may differ from the reference program's by a relative error of at most 0.0093.
Values may be sent and summed in bfloat16 or wider, within the bound.
No kernel may reach another device: no remote copies, remote signals or barrier semaphores. Data moves between devices by JAX's collectives and lax.ppermute only.
A program may use at most 128 MiB of HBM per device.

```python
import math
import jax
import jax.numpy as jnp
from jax import lax

NUM_VARIABLES = 16
HID = 128
NUM_MERIDIANS = 1440
LAT_DEV = 4
P_DEV = 256
ENSEMBLE_SIZE = 128
NUM_PARALLELS = 64
P_SIZE = 4096


def draw_obs_count(key, part):
    tiles = P_SIZE // P_DEV
    counts = jax.random.randint(key, (tiles,), P_DEV // 2, P_DEV + 1)
    full_tile = jax.random.randint(jax.random.fold_in(key, 17), (), 0, tiles)
    return jnp.where(jnp.arange(tiles) == full_tile, P_DEV, counts).astype(jnp.int32)


def place_ends(values, stream_key, smallest, largest):
    longest = values.shape.index(max(values.shape))
    spots = []
    for shift in (0, 1):
        where = [jax.random.randint(jax.random.fold_in(stream_key, axis), (), 0, length) for axis, length in enumerate(values.shape)]
        where[longest] = (where[longest] + shift) % values.shape[longest]
        spots.append(tuple(where))
    return values.at[spots[0]].set(smallest).at[spots[1]].set(largest)


def level_of(key, extent, split, least, top_value):
    gain, own = 1.0, jax.random.fold_in(key, 6)
    for axis_at, parts in split:
        steps = jnp.exp(jax.random.uniform(jax.random.fold_in(own, axis_at), (parts,), jnp.float32, least / len(split), top_value / len(split)))
        gain = gain * jnp.repeat(steps, extent[axis_at] // parts).reshape([-1 if axis == axis_at else 1 for axis in range(len(extent))])
    return gain


def gaussian(key, dims, deviation, limit, split=(), held_as=jnp.bfloat16):
    array = jax.random.normal(key, dims, jnp.float32) * deviation
    if len(split) > 0:
        array = level_of(key, dims, split, -0.22, 0.18) * array
    return jnp.clip(array, min=-limit, max=limit).astype(held_as)


def setup_inputs(seed: int = 0) -> dict:
    seeds = jax.random.split(jax.random.key(seed), 10)
    return {
        "ensemble_weather": gaussian(seeds[0], (ENSEMBLE_SIZE, NUM_VARIABLES, NUM_PARALLELS, NUM_MERIDIANS), 1.0, 6.0, ((0, 8), (2, 16))),
        "conv_in": gaussian(seeds[1], (HID, NUM_VARIABLES, 3, 3), (9 * NUM_VARIABLES) ** -0.5, 0.5),
        "bias_in": gaussian(seeds[2], (HID,), 0.5, 3.0, (), jnp.float32),
        "conv_out": gaussian(seeds[3], (NUM_VARIABLES, HID, 3, 3), (9 * HID) ** -0.5, 0.1875),
        "bias_out": gaussian(seeds[4], (NUM_VARIABLES,), 0.5, 3.0, (), jnp.float32),
        "observed_entry_index": place_ends(jax.random.randint(seeds[5], (P_SIZE,), 0, NUM_VARIABLES * LAT_DEV * NUM_MERIDIANS), jax.random.fold_in(seeds[5], 1), 0, (NUM_VARIABLES * LAT_DEV * NUM_MERIDIANS) - 1).astype(jnp.int32),
        "obs_count": draw_obs_count(jax.random.fold_in(seeds[9], 71), 0),
        "obs_value": gaussian(seeds[7], (P_SIZE,), 1.5, 8.0, ((0, 16),), jnp.float32),
        "obs_sigma": jnp.clip(jnp.exp(math.log(2.0) - 1.3862944 * jax.random.uniform(seeds[8], (P_SIZE,), jnp.float32) ** level_of(seeds[8], (P_SIZE,), ((0, 16),), -0.2, 0.2)), 0.5, 2.0),
    }


def convolve(field, kernel):
    wrapped = jnp.concatenate([field[..., -1:], field, field[..., :1]], axis=-1)
    padded = jnp.pad(wrapped, ((0, 0), (0, 0), (1, 1), (0, 0)))
    return lax.conv_general_dilated(padded.astype(jnp.float32), kernel.astype(jnp.float32), (1, 1), 'VALID', dimension_numbers=('NCHW', 'OIHW', 'NCHW'), precision=lax.Precision.HIGHEST)

def reference(ensemble_weather, conv_in, bias_in, conv_out, bias_out, observed_entry_index, obs_count, obs_value, obs_sigma):

    def propagate_realization(member):
        inner = convolve(member[None], conv_in)[0] + bias_in[:, None, None]
        hidden = jax.nn.silu(inner).astype(jnp.bfloat16)
        outer = convolve(hidden[None], conv_out)[0] + bias_out[:, None, None]
        return (member.astype(jnp.float32) + outer).astype(jnp.bfloat16)
    predicted_weather = lax.map(propagate_realization, ensemble_weather)
    cells = LAT_DEV * NUM_MERIDIANS
    tiles = jnp.arange(P_SIZE, dtype=jnp.int32) // P_DEV
    field_no = observed_entry_index // cells
    rest = observed_entry_index % cells
    row_no = rest // NUM_MERIDIANS
    col_no = rest % NUM_MERIDIANS
    linear_vector = field_no * (NUM_PARALLELS * NUM_MERIDIANS) + (tiles * LAT_DEV + row_no) * NUM_MERIDIANS + col_no
    measurement_vector = predicted_weather.reshape(ENSEMBLE_SIZE, NUM_VARIABLES * NUM_PARALLELS * NUM_MERIDIANS)[:, linear_vector.astype(jnp.int32)].astype(jnp.float32)
    live = (jnp.arange(P_SIZE, dtype=jnp.int32) % P_DEV < obs_count[tiles]).astype(jnp.float32)
    mean_obs = lax.optimization_barrier(jnp.sum(measurement_vector, axis=0)) / ENSEMBLE_SIZE
    anomalies = (measurement_vector - mean_obs[None, :]) * (live / (obs_sigma * math.sqrt(ENSEMBLE_SIZE - 1)))[None, :]
    innov = live * (obs_value - mean_obs) / obs_sigma
    eye = jnp.eye(ENSEMBLE_SIZE, dtype=jnp.float32)
    gram = jnp.dot(anomalies, anomalies.T, precision=lax.Precision.HIGHEST) + eye
    factor = jnp.linalg.cholesky(gram)
    proj = jnp.dot(anomalies, innov, precision=lax.Precision.HIGHEST)
    middle = jax.scipy.linalg.solve_triangular(factor, proj, lower=True)
    mean_weights = jax.scipy.linalg.solve_triangular(factor, middle, lower=True, trans='T') / math.sqrt(ENSEMBLE_SIZE - 1)
    inverse_t = jax.scipy.linalg.solve_triangular(factor, eye, lower=True, trans='T')
    coeff = mean_weights[:, None] + inverse_t
    transform = (coeff - lax.optimization_barrier(jnp.mean(coeff, axis=0, keepdims=True)) + 1.0 / ENSEMBLE_SIZE).astype(jnp.bfloat16)

    def update_field(sensor_position):
        variable_grid = lax.dynamic_index_in_dim(predicted_weather, sensor_position, 1, keepdims=False).reshape(ENSEMBLE_SIZE, NUM_PARALLELS * NUM_MERIDIANS)
        mixed = jnp.dot(transform.T.astype(jnp.float32), variable_grid.astype(jnp.float32), preferred_element_type=jnp.float32)
        return mixed.astype(jnp.bfloat16).reshape(ENSEMBLE_SIZE, NUM_PARALLELS, NUM_MERIDIANS)
    planes = lax.map(update_field, jnp.arange(NUM_VARIABLES, dtype=jnp.int32))
    analysis = jnp.transpose(planes, (1, 0, 2, 3))
    return (analysis, factor, mean_weights)
```

```python
import math

import jax
import jax.numpy as jnp
from jax import lax
from jax.experimental import pallas as pl
from jax.experimental.pallas import tpu as pltpu
from jax.sharding import PartitionSpec as P

FIELDS = 16
HID = 128
ROWS = 4
LON = 1440
RING = 1536
SLOTS = 256
GROUP = 16
PLANES = ROWS * FIELDS * GROUP
N_ENS = 8
MEMBERS = 128
VMEM_LIMIT = 56 * 1024 * 1024


def forecast_kernel(
    index_ref,
    x_ref,
    top_ref,
    bottom_ref,
    first_top_ref,
    first_bottom_ref,
    second_ref,
    bias_ref,
    fields_ref,
    observed_ref,
    held_ref,
):
    member = pl.program_id(0)
    main = x_ref[0].reshape(ROWS * FIELDS, LON)
    stack = jnp.concatenate(
        [top_ref[0].reshape(2 * FIELDS, LON), main, bottom_ref[0].reshape(2 * FIELDS, LON)],
        axis=0,
    )
    ring = jnp.concatenate([stack, stack[:, :64], stack[:, LON - 32 :]], axis=1)
    left = pltpu.roll(ring, 1, 1)
    right = pltpu.roll(ring, RING - 1, 1)
    ones = jnp.ones((16, RING), jnp.bfloat16)

    def hidden_rows(low, weights_ref):
        high = low + 5 * FIELDS
        taps = jnp.concatenate([left[low:high], ring[low:high], right[low:high], ones], axis=0)
        half = jnp.dot(weights_ref[...], taps, preferred_element_type=jnp.float32)
        return (half * jnp.tanh(half) + half).astype(jnp.bfloat16)

    hidden = jnp.concatenate(
        [hidden_rows(0, first_top_ref), hidden_rows(3 * FIELDS, first_bottom_ref)], axis=0
    )
    outer = jnp.dot(second_ref[...], hidden, preferred_element_type=jnp.float32)
    count = ROWS * FIELDS
    change = (
        pltpu.roll(outer[:count], 1, 1)
        + outer[count : 2 * count]
        + pltpu.roll(outer[2 * count :], RING - 1, 1)
    )
    base = main.astype(jnp.float32) + bias_ref[...]
    own = jnp.concatenate([base, base[:, : RING - LON]], axis=1) + change
    for tile in range(RING // 128):
        held_ref[pl.ds(tile * PLANES + member, count, stride=GROUP), :] = own[
            :, tile * 128 : (tile + 1) * 128
        ]

    @pl.when(member == pl.num_programs(0) - 1)
    def _():
        for field in range(FIELDS):
            for row in range(ROWS):
                at = (row * FIELDS + field) * GROUP
                for tile in range(RING // 128):
                    low, high = tile * 128, min(tile * 128 + 128, LON)
                    fields_ref[field // 2, (field % 2) * ROWS + row, :, low:high] = held_ref[
                        tile * PLANES + at : tile * PLANES + at + GROUP, : high - low
                    ].astype(jnp.bfloat16)
        lane = lax.broadcasted_iota(jnp.int32, (GROUP, 128), 1)
        for part in range(SLOTS // 128):

            def pick(slot, total):
                entry = index_ref[part * 128 + slot]
                plane = entry // LON
                column = entry - plane * LON
                at = (column // 128) * PLANES
                at += ((plane % ROWS) * FIELDS + plane // ROWS) * GROUP
                block = held_ref[pl.ds(pl.multiple_of(at, GROUP), GROUP), :]
                moved = pltpu.roll(block, (slot - column + 128 * 16) % 128, 1)
                return jnp.where(lane == slot, moved, total)

            total = lax.fori_loop(
                0, 128, pick, jnp.zeros((GROUP, 128), jnp.float32), unroll=8
            )
            observed_ref[:, part * 128 : (part + 1) * 128] = total.astype(jnp.bfloat16)


def forecast(index, own, top, bottom, first_top, first_bottom, second, bias):
    whole = lambda *shape: pl.BlockSpec(shape, lambda m, *_: (0,) * len(shape))
    return pl.pallas_call(
        forecast_kernel,
        grid_spec=pltpu.PrefetchScalarGridSpec(
            num_scalar_prefetch=1,
            grid=(GROUP,),
            in_specs=[
                pl.BlockSpec((1, ROWS, FIELDS, LON), lambda m, *_: (m, 0, 0, 0)),
                pl.BlockSpec((1, 2, FIELDS, LON), lambda m, *_: (m, 0, 0, 0)),
                pl.BlockSpec((1, 2, FIELDS, LON), lambda m, *_: (m, 0, 0, 0)),
                whole(*first_top.shape),
                whole(*first_bottom.shape),
                whole(*second.shape),
                whole(*bias.shape),
            ],
            out_specs=[whole(N_ENS, 8, GROUP, LON), whole(GROUP, SLOTS)],
            scratch_shapes=[pltpu.VMEM((RING // 128 * PLANES, 128), jnp.float32)],
        ),
        out_shape=[
            jax.ShapeDtypeStruct((N_ENS, 8, GROUP, LON), jnp.bfloat16),
            jax.ShapeDtypeStruct((GROUP, SLOTS), jnp.bfloat16),
        ],
        compiler_params=pltpu.CompilerParams(vmem_limit_bytes=VMEM_LIMIT),
    )(index, own, top, bottom, first_top, first_bottom, second, bias)


def products_kernel(observed_ref, count_ref, value_ref, sigma_ref, out_ref):
    observed = observed_ref[...].astype(jnp.float32)
    mean = jnp.sum(observed, axis=0, keepdims=True) / MEMBERS
    slot = lax.broadcasted_iota(jnp.int32, (1, SLOTS), 1)
    live = (slot < count_ref[0]).astype(jnp.float32)
    sigma = sigma_ref[...]
    anomalies = (observed - mean) * (live / (sigma * math.sqrt(MEMBERS - 1)))
    innov = live * (value_ref[...] - mean) / sigma
    left = jnp.concatenate([anomalies, jnp.broadcast_to(innov, (8, SLOTS))], axis=0)
    out_ref[...] = lax.dot_general(
        left,
        anomalies,
        (((1,), (1,)), ((), ())),
        precision=lax.Precision.HIGHEST,
        preferred_element_type=jnp.float32,
    )


def products(observed, count, value, sigma):
    vmem = pl.BlockSpec(memory_space=pltpu.VMEM)
    return pl.pallas_call(
        products_kernel,
        in_specs=[vmem, pl.BlockSpec(memory_space=pltpu.SMEM), vmem, vmem],
        out_specs=vmem,
        out_shape=jax.ShapeDtypeStruct((MEMBERS + 8, MEMBERS), jnp.float32),
    )(observed, count, value.reshape(1, SLOTS), sigma.reshape(1, SLOTS))


def transform_kernel(products_ref, factor_ref, weights_ref, transform_ref):
    n = MEMBERS
    row = lax.broadcasted_iota(jnp.int32, (n, n), 0)
    column = lax.broadcasted_iota(jnp.int32, (n, n), 1)
    eye = (row == column).astype(jnp.float32)
    gram = products_ref[0:n, :] + eye
    blocks = [
        [gram[b : b + 8], eye[b : b + 8]] for b in range(0, n, 8)
    ]
    within = lax.broadcasted_iota(jnp.int32, (8, n), 0)
    for b in range(n // 8):
        upper, inverse = blocks[b]
        for k in range(8):
            j = 8 * b + k
            scale = lax.rsqrt(upper[k : k + 1, j : j + 1])
            share = upper[:, j : j + 1] * scale
            upper_row = upper[k : k + 1] * scale
            inverse_row = inverse[k : k + 1] * scale
            share = jnp.where(within > k, share, 0.0)
            upper = jnp.where(within == k, upper_row, upper - share * upper_row)
            inverse = jnp.where(within == k, inverse_row, inverse - share * inverse_row)
        blocks[b] = [upper, inverse]
        turned = upper.T
        for t in range(b + 1, n // 8):
            later_upper, later_inverse = blocks[t]
            for k in range(8):
                share = turned[8 * t : 8 * t + 8, k : k + 1]
                later_upper = later_upper - share * upper[k : k + 1]
                later_inverse = later_inverse - share * inverse[k : k + 1]
            blocks[t] = [later_upper, later_inverse]
    upper = jnp.concatenate([pair[0] for pair in blocks], axis=0)
    inverse = jnp.concatenate([pair[1] for pair in blocks], axis=0)
    factor_ref[...] = jnp.where(row <= column, upper, 0.0).T
    proj = products_ref[n : n + 1, :]
    middle = jnp.sum(inverse * proj, axis=1, keepdims=True)
    weights = jnp.sum(inverse * middle, axis=0, keepdims=True) / math.sqrt(n - 1)
    weights_ref[...] = weights
    coeff = inverse + weights
    transform = coeff - jnp.mean(coeff, axis=1, keepdims=True) + 1.0 / n
    transform_ref[...] = transform.astype(jnp.bfloat16)


def transform_of(summed):
    vmem = pl.BlockSpec(memory_space=pltpu.VMEM)
    return pl.pallas_call(
        transform_kernel,
        in_specs=[vmem],
        out_specs=[vmem, vmem, vmem],
        out_shape=[
            jax.ShapeDtypeStruct((MEMBERS, MEMBERS), jnp.float32),
            jax.ShapeDtypeStruct((1, MEMBERS), jnp.float32),
            jax.ShapeDtypeStruct((MEMBERS, MEMBERS), jnp.bfloat16),
        ],
    )(summed)


def update_kernel(transform_ref, fields_ref, out_ref):
    fields = fields_ref[:, 0].reshape(MEMBERS, LON)
    mixed = jnp.dot(transform_ref[...], fields, preferred_element_type=jnp.float32)
    out_ref[:, 0] = mixed.astype(jnp.bfloat16).reshape(N_ENS, GROUP, LON)


def update(transform, fields):
    block = pl.BlockSpec((N_ENS, 1, GROUP, LON), lambda k: (0, k, 0, 0))
    return pl.pallas_call(
        update_kernel,
        grid=(8,),
        in_specs=[pl.BlockSpec((MEMBERS, MEMBERS), lambda k: (0, 0)), block],
        out_specs=block,
        out_shape=jax.ShapeDtypeStruct((N_ENS, 8, GROUP, LON), jnp.bfloat16),
    )(transform, fields)


def first_weights(conv_in, bias_in, mask):
    kernel = conv_in.astype(jnp.float32) * 0.5
    by_tap = jnp.transpose(kernel, (0, 3, 2, 1))
    placed = [
        jnp.pad(by_tap, ((0, 0), (0, 0), (r, 2 - r), (0, 0))).reshape(HID, 15 * FIELDS)
        for r in range(3)
    ]
    half = bias_in * 0.5
    high = half.astype(jnp.bfloat16).astype(jnp.float32)
    middle = (half - high).astype(jnp.bfloat16).astype(jnp.float32)
    low = half - high - middle
    bias = jnp.pad(jnp.stack([high, middle, low], axis=1), ((0, 0), (0, 13)))
    rows = [jnp.concatenate([part, bias], axis=1) * mask[r] for r, part in enumerate(placed)]
    return jnp.concatenate(rows, axis=0).astype(jnp.bfloat16)


def second_weights(conv_out):
    by_tap = jnp.transpose(conv_out, (3, 0, 2, 1))
    placed = [jnp.pad(by_tap, ((0, 0), (0, 0), (r, 3 - r), (0, 0))) for r in range(ROWS)]
    return jnp.stack(placed, axis=1).reshape(3 * ROWS * FIELDS, 6 * HID)


def on_device(
    ensemble_weather,
    conv_in,
    bias_in,
    conv_out,
    bias_out,
    observed_entry_index,
    obs_count,
    obs_value,
    obs_sigma,
):
    tiles = lax.axis_size("map")
    tile = lax.axis_index("map")
    down = [(i, i + 1) for i in range(tiles - 1)]
    up = [(i + 1, i) for i in range(tiles - 1)]
    own = jnp.transpose(ensemble_weather, (0, 2, 1, 3))
    top = lax.ppermute(own[:, ROWS - 2 :], "map", down)
    bottom = lax.ppermute(own[:, :2], "map", up)
    one = jnp.float32(1.0)
    inner_top = (tile > 0).astype(jnp.float32)
    inner_bottom = (tile < tiles - 1).astype(jnp.float32)
    first_top = first_weights(conv_in, bias_in, [inner_top, one, one])
    first_bottom = first_weights(conv_in, bias_in, [one, one, inner_bottom])
    second = second_weights(conv_out)
    bias = jnp.tile(bias_out, ROWS).reshape(ROWS * FIELDS, 1)
    fields, observed = forecast(
        observed_entry_index, own, top, bottom, first_top, first_bottom, second, bias
    )
    observed = lax.all_gather(observed, "ens", axis=0, tiled=True)
    gathered = lax.all_to_all(fields, "ens", split_axis=0, concat_axis=0, tiled=True)
    summed = lax.psum(products(observed, obs_count, obs_value, obs_sigma), "map")
    factor, mean_weights, transform = transform_of(summed)
    mixed = update(transform, gathered)
    back = lax.all_to_all(mixed, "ens", split_axis=0, concat_axis=0, tiled=True)
    analysis = jnp.transpose(back.reshape(FIELDS, ROWS, GROUP, LON), (2, 0, 1, 3))
    return (analysis, factor, mean_weights.reshape(MEMBERS))


def solution(mesh):
    placed = (
        P("ens", None, "map", None),
        P(),
        P(),
        P(),
        P(),
        P("map"),
        P("map"),
        P("map"),
        P("map"),
    )
    return jax.shard_map(
        on_device,
        mesh=mesh,
        in_specs=placed,
        out_specs=(P("ens", None, "map", None), P(), P()),
        check_vma=False,
    )
```

```python
import functools
import math

import jax
import jax.numpy as jnp
from jax import lax
from jax.experimental import pallas as pl
from jax.experimental.pallas import tpu as pltpu
from jax.sharding import PartitionSpec as P

FIELDS = 16
HID = 128
ROWS = 4
LON = 1440
RING = 1536
SLOTS = 256
GROUP = 16
PLANES = ROWS * FIELDS
CHUNKS = 4
N_ENS = 8
MEMBERS = 128
VMEM_LIMIT = 56 * 1024 * 1024


def forecast_kernel(
    x_ref,
    top_ref,
    bottom_ref,
    first_top_ref,
    first_bottom_ref,
    second_ref,
    bias_ref,
    column_ref,
    plane_ref,
    earlier_ref,
    held_ref,
    fields_ref,
    observed_ref,
    *,
    start,
):
    del held_ref
    member = pl.program_id(0)
    main = x_ref[0].reshape(PLANES, LON)
    stack = jnp.concatenate(
        [top_ref[0].reshape(2 * FIELDS, LON), main, bottom_ref[0].reshape(2 * FIELDS, LON)],
        axis=0,
    )
    ring = jnp.concatenate([stack, stack[:, :64], stack[:, LON - 32 :]], axis=1)
    left = pltpu.roll(ring, 1, 1)
    right = pltpu.roll(ring, RING - 1, 1)
    ones = jnp.ones((16, RING), jnp.bfloat16)

    def hidden_rows(low, weights_ref):
        high = low + 5 * FIELDS
        taps = jnp.concatenate([left[low:high], ring[low:high], right[low:high], ones], axis=0)
        half = jnp.dot(weights_ref[...], taps, preferred_element_type=jnp.float32)
        return (half * jnp.tanh(half) + half).astype(jnp.bfloat16)

    hidden = jnp.concatenate(
        [hidden_rows(0, first_top_ref), hidden_rows(3 * FIELDS, first_bottom_ref)], axis=0
    )
    outer = jnp.dot(second_ref[...], hidden, preferred_element_type=jnp.float32)
    change = (
        pltpu.roll(outer[:PLANES], 1, 1)
        + outer[PLANES : 2 * PLANES]
        + pltpu.roll(outer[2 * PLANES :], RING - 1, 1)
    )
    base = ring[2 * FIELDS : 2 * FIELDS + PLANES].astype(jnp.float32) + bias_ref[...]
    own = (base + change).astype(jnp.bfloat16)
    fields_ref[:, 0] = own[:, :LON].reshape(N_ENS, 8, LON)
    picked = jnp.dot(own, column_ref[...], preferred_element_type=jnp.float32)
    here = lax.broadcasted_iota(jnp.int32, (PLANES, SLOTS), 0) == plane_ref[...]

    @pl.when(member == 0)
    def _():
        observed_ref[...] = earlier_ref[...]

    observed_ref[pl.ds(start + member, 1), :] = jnp.sum(
        jnp.where(here, picked, 0.0), axis=0, keepdims=True
    )


def cost(microseconds):
    return pl.CostEstimate(
        flops=int(microseconds * 1e9), transcendentals=0, bytes_accessed=int(microseconds * 1e6)
    )


def forecast(start, own, top, bottom, *shared, fields):
    count = top.shape[0]
    whole = lambda array: pl.BlockSpec(array.shape, lambda m: (0,) * array.ndim)
    in_specs = [
        pl.BlockSpec((1, ROWS, FIELDS, LON), lambda m: (start + m, 0, 0, 0)),
        pl.BlockSpec((1, 2, FIELDS, LON), lambda m: (m, 0, 0, 0)),
        pl.BlockSpec((1, 2, FIELDS, LON), lambda m: (m, 0, 0, 0)),
    ]
    in_specs += [whole(array) for array in shared] + [pl.BlockSpec(memory_space=pl.ANY)]
    arrays = [own, top, bottom, *shared, fields]
    kernel = functools.partial(forecast_kernel, start=start)
    aliases = {len(arrays) - 1: 0}
    if fields is None:
        arrays, in_specs, aliases = arrays[:-1], in_specs[:-1], {}
        kernel = lambda *refs: forecast_kernel(*refs[:-2], None, *refs[-2:], start=start)
    return pl.pallas_call(
        kernel,
        grid=(count,),
        in_specs=in_specs,
        out_specs=[
            pl.BlockSpec((N_ENS, 1, 8, LON), lambda m: (0, start + m, 0, 0)),
            pl.BlockSpec((GROUP, SLOTS), lambda m: (0, 0)),
        ],
        out_shape=[
            jax.ShapeDtypeStruct((N_ENS, GROUP, 8, LON), jnp.bfloat16),
            jax.ShapeDtypeStruct((GROUP, SLOTS), jnp.float32),
        ],
        input_output_aliases=aliases,
        cost_estimate=cost(10),
        compiler_params=pltpu.CompilerParams(vmem_limit_bytes=VMEM_LIMIT),
    )(*arrays)


def products_kernel(place_ref, count_ref, value_ref, sigma_ref, *refs):
    pieces, out_ref, held_ref = refs[:N_ENS], refs[N_ENS], refs[N_ENS + 1]
    for step, piece in enumerate(pieces):
        at = pl.multiple_of(place_ref[step] * GROUP, GROUP)
        held_ref[pl.ds(at, GROUP), :] = piece[...]
    observed = held_ref[...]
    mean = jnp.sum(observed, axis=0, keepdims=True) / MEMBERS
    slot = lax.broadcasted_iota(jnp.int32, (1, SLOTS), 1)
    live = (slot < count_ref[0]).astype(jnp.float32)
    sigma = sigma_ref[...]
    anomalies = (observed - mean) * (live / (sigma * math.sqrt(MEMBERS - 1)))
    innov = live * (value_ref[...] - mean) / sigma
    left = jnp.concatenate([anomalies, jnp.broadcast_to(innov, (8, SLOTS))], axis=0)
    out_ref[...] = lax.dot_general(
        left,
        anomalies,
        (((1,), (1,)), ((), ())),
        precision=lax.Precision.HIGHEST,
        preferred_element_type=jnp.float32,
    )


def products(pieces, places, count, value, sigma):
    vmem = pl.BlockSpec(memory_space=pltpu.VMEM)
    smem = pl.BlockSpec(memory_space=pltpu.SMEM)
    return pl.pallas_call(
        products_kernel,
        in_specs=[smem, smem] + [vmem] * (2 + N_ENS),
        out_specs=vmem,
        out_shape=jax.ShapeDtypeStruct((MEMBERS + 8, MEMBERS), jnp.float32),
        cost_estimate=cost(2),
        scratch_shapes=[pltpu.VMEM((MEMBERS, SLOTS), jnp.float32)],
    )(places, count, value.reshape(1, SLOTS), sigma.reshape(1, SLOTS), *pieces)


def transform_kernel(a_ref, b_ref, c_ref, d_ref, factor_ref, weights_ref, transform_ref):
    n = MEMBERS
    total = (a_ref[...] + b_ref[...]) + (c_ref[...] + d_ref[...])
    row = lax.broadcasted_iota(jnp.int32, (n, n), 0)
    column = lax.broadcasted_iota(jnp.int32, (n, n), 1)
    eye = (row == column).astype(jnp.float32)
    gram = total[0:n] + eye
    blocks = [
        [gram[b : b + 8], eye[b : b + 8]] for b in range(0, n, 8)
    ]
    within = lax.broadcasted_iota(jnp.int32, (8, n), 0)
    for b in range(n // 8):
        upper, inverse = blocks[b]
        for k in range(8):
            j = 8 * b + k
            scale = lax.rsqrt(upper[k : k + 1, j : j + 1])
            share = upper[:, j : j + 1] * scale
            upper_row = upper[k : k + 1] * scale
            inverse_row = inverse[k : k + 1] * scale
            share = jnp.where(within > k, share, 0.0)
            upper = jnp.where(within == k, upper_row, upper - share * upper_row)
            inverse = jnp.where(within == k, inverse_row, inverse - share * inverse_row)
        blocks[b] = [upper, inverse]
        turned = upper.T
        for t in range(b + 1, n // 8):
            later_upper, later_inverse = blocks[t]
            for k in range(8):
                share = turned[8 * t : 8 * t + 8, k : k + 1]
                later_upper = later_upper - share * upper[k : k + 1]
                later_inverse = later_inverse - share * inverse[k : k + 1]
            blocks[t] = [later_upper, later_inverse]
    upper = jnp.concatenate([pair[0] for pair in blocks], axis=0)
    inverse = jnp.concatenate([pair[1] for pair in blocks], axis=0)
    factor_ref[...] = jnp.where(row <= column, upper, 0.0).T
    proj = total[n : n + 1]
    middle = jnp.sum(inverse * proj, axis=1, keepdims=True)
    weights = jnp.sum(inverse * middle, axis=0, keepdims=True) / math.sqrt(n - 1)
    weights_ref[...] = weights
    coeff = inverse + weights
    transform = coeff - jnp.mean(coeff, axis=1, keepdims=True) + 1.0 / n
    transform_ref[...] = transform.astype(jnp.bfloat16)


def transform_of(parts):
    vmem = pl.BlockSpec(memory_space=pltpu.VMEM)
    return pl.pallas_call(
        transform_kernel,
        in_specs=[vmem] * 4,
        out_specs=[vmem, vmem, vmem],
        out_shape=[
            jax.ShapeDtypeStruct((MEMBERS, MEMBERS), jnp.float32),
            jax.ShapeDtypeStruct((1, MEMBERS), jnp.float32),
            jax.ShapeDtypeStruct((MEMBERS, MEMBERS), jnp.bfloat16),
        ],
        cost_estimate=cost(12),
    )(*parts)


def update_kernel(transform_ref, fields_ref, out_ref, spread_ref):
    rows = MEMBERS * 8

    @pl.when(pl.program_id(0) == 0)
    def _():
        member = lax.broadcasted_iota(jnp.int32, (rows, MEMBERS), 0) // 8
        column = lax.broadcasted_iota(jnp.int32, (rows, MEMBERS), 1)
        repeat = (member == column).astype(jnp.bfloat16)
        tall = jnp.dot(repeat, transform_ref[...], preferred_element_type=jnp.float32)
        wide = lax.dot_general(
            tall.astype(jnp.bfloat16),
            repeat,
            (((1,), (1,)), ((), ())),
            preferred_element_type=jnp.float32,
        )
        plane = lax.broadcasted_iota(jnp.int32, (rows, rows), 0) % 8
        same = plane == lax.broadcasted_iota(jnp.int32, (rows, rows), 1) % 8
        spread_ref[...] = jnp.where(same, wide, 0.0).astype(jnp.bfloat16)

    mixed = jnp.dot(spread_ref[...], fields_ref[...], preferred_element_type=jnp.float32)
    out_ref[...] = mixed.astype(jnp.bfloat16)


def update(transform, fields):
    rows = MEMBERS * 8
    block = pl.BlockSpec((rows, 256), lambda k: (0, k))
    return pl.pallas_call(
        update_kernel,
        grid=(RING // 256,),
        in_specs=[pl.BlockSpec((MEMBERS, MEMBERS), lambda k: (0, 0)), block],
        out_specs=block,
        out_shape=jax.ShapeDtypeStruct((rows, LON), jnp.bfloat16),
        scratch_shapes=[pltpu.VMEM((rows, rows), jnp.bfloat16)],
        cost_estimate=cost(6),
        compiler_params=pltpu.CompilerParams(vmem_limit_bytes=VMEM_LIMIT),
    )(transform, fields.reshape(rows, LON)).reshape(fields.shape)


def first_weights(conv_in, bias_in, mask):
    kernel = conv_in.astype(jnp.float32) * 0.5
    by_tap = jnp.transpose(kernel, (0, 3, 2, 1))
    placed = [
        jnp.pad(by_tap, ((0, 0), (0, 0), (r, 2 - r), (0, 0))).reshape(HID, 15 * FIELDS)
        for r in range(3)
    ]
    half = bias_in * 0.5
    high = half.astype(jnp.bfloat16).astype(jnp.float32)
    middle = (half - high).astype(jnp.bfloat16).astype(jnp.float32)
    low = half - high - middle
    bias = jnp.pad(jnp.stack([high, middle, low], axis=1), ((0, 0), (0, 13)))
    rows = [jnp.concatenate([part, bias], axis=1) * mask[r] for r, part in enumerate(placed)]
    return jnp.concatenate(rows, axis=0).astype(jnp.bfloat16)


def second_weights(conv_out):
    by_tap = jnp.transpose(conv_out, (3, 0, 2, 1))
    placed = [jnp.pad(by_tap, ((0, 0), (0, 0), (r, 3 - r), (0, 0))) for r in range(ROWS)]
    return jnp.stack(placed, axis=1).reshape(3 * ROWS * FIELDS, 6 * HID)


def on_device(
    ensemble_weather,
    conv_in,
    bias_in,
    conv_out,
    bias_out,
    observed_entry_index,
    obs_count,
    obs_value,
    obs_sigma,
):
    tiles = lax.axis_size("map")
    tile = lax.axis_index("map")
    own_place = lax.axis_index("ens")
    down = [(i, i + 1) for i in range(tiles - 1)]
    up = [(i + 1, i) for i in range(tiles - 1)]

    def swap(value, axis, step):
        pairs = [(i, i ^ step) for i in range(lax.axis_size(axis))]
        return lax.ppermute(value, axis, pairs)

    own = jnp.transpose(ensemble_weather, (0, 2, 1, 3))
    share = GROUP // CHUNKS
    halos = []
    for chunk in range(CHUNKS):
        part = own[chunk * share : (chunk + 1) * share]
        edges = (part[:, ROWS - 2 :], part[:, :2])
        if halos:
            edges, halos[-1] = lax.optimization_barrier((edges, halos[-1]))
        halos.append((lax.ppermute(edges[0], "map", down), lax.ppermute(edges[1], "map", up)))
    one = jnp.float32(1.0)
    inner_top = (tile > 0).astype(jnp.float32)
    inner_bottom = (tile < tiles - 1).astype(jnp.float32)
    first_top = first_weights(conv_in, bias_in, [inner_top, one, one])
    first_bottom = first_weights(conv_in, bias_in, [one, one, inner_bottom])
    second = second_weights(conv_out)
    bias = jnp.tile(bias_out, ROWS).reshape(PLANES, 1)
    plane = observed_entry_index // LON
    column = observed_entry_index - plane * LON
    picks = (jnp.arange(RING)[:, None] == column[None, :]).astype(jnp.bfloat16)
    plane = ((plane % ROWS) * FIELDS + plane // ROWS).reshape(1, SLOTS)

    exchange = lambda value: lax.all_to_all(
        value, "ens", split_axis=0, concat_axis=0, tiled=True
    )
    fields, observed = None, jnp.zeros((GROUP, SLOTS), jnp.float32)
    for chunk, (top, bottom) in enumerate(halos):
        fields, observed = forecast(
            chunk * share,
            own,
            top,
            bottom,
            first_top,
            first_bottom,
            second,
            bias,
            picks,
            plane,
            observed,
            fields=fields,
        )
    pieces = [observed] + [swap(observed, "ens", step) for step in range(1, N_ENS)]
    places = jnp.bitwise_xor(own_place, jnp.arange(N_ENS, dtype=jnp.int32))
    pieces, fields = lax.optimization_barrier((pieces, fields))
    gathered = exchange(fields)
    part = products(pieces, places, obs_count, obs_value, obs_sigma)
    near = [part] + [swap(part, "map", step) for step in (1, 2, 3)]
    row = (near[0] + near[1]) + (near[2] + near[3])
    factor, mean_weights, transform = transform_of(
        [row] + [swap(row, "map", step) for step in (4, 8, 12)]
    )
    back = exchange(update(transform, gathered))
    back = back.reshape(ROWS, 2, GROUP, 8, LON)
    analysis = jnp.transpose(back, (2, 1, 3, 0, 4)).reshape(GROUP, FIELDS, ROWS, LON)
    return (analysis, factor, mean_weights.reshape(MEMBERS))


def solution(mesh):
    placed = (
        P("ens", None, "map", None),
        P(),
        P(),
        P(),
        P(),
        P("map"),
        P("map"),
        P("map"),
        P("map"),
    )
    return jax.shard_map(
        on_device,
        mesh=mesh,
        in_specs=placed,
        out_specs=(P("ens", None, "map", None), P(), P()),
        check_vma=False,
    )
```

```python
import functools
import math

import jax
import jax.numpy as jnp
from jax import lax
from jax.experimental import pallas as pl
from jax.experimental.pallas import tpu as pltpu
from jax.sharding import PartitionSpec as P

FIELDS = 16
HID = 128
ROWS = 4
LON = 1440
RING = 1536
SLOTS = 256
GROUP = 16
PLANES = ROWS * FIELDS
CHUNKS = 2
N_ENS = 8
MEMBERS = 128
VMEM_LIMIT = 56 * 1024 * 1024


def forecast_kernel(
    x_ref,
    top_ref,
    bottom_ref,
    first_top_ref,
    first_bottom_ref,
    second_low_ref,
    second_middle_ref,
    second_high_ref,
    bias_ref,
    column_ref,
    plane_ref,
    fields_ref,
    observed_ref,
    held_ref,
):
    member = pl.program_id(0)
    main = x_ref[0].reshape(PLANES, LON)
    stack = jnp.concatenate(
        [top_ref[0].reshape(2 * FIELDS, LON), main, bottom_ref[0].reshape(2 * FIELDS, LON)],
        axis=0,
    )
    ring = jnp.concatenate([stack, stack[:, :64], stack[:, LON - 32 :]], axis=1)
    left = pltpu.roll(ring, 1, 1)
    right = pltpu.roll(ring, RING - 1, 1)
    ones = jnp.ones((16, RING), jnp.bfloat16)

    def hidden_rows(low, weights_ref):
        high = low + 5 * FIELDS
        taps = jnp.concatenate([left[low:high], ring[low:high], right[low:high], ones], axis=0)
        half = jnp.dot(weights_ref[...], taps, preferred_element_type=jnp.float32)
        return (half * jnp.tanh(half) + half).astype(jnp.bfloat16)

    hidden = jnp.concatenate(
        [hidden_rows(0, first_top_ref), hidden_rows(3 * FIELDS, first_bottom_ref)], axis=0
    )

    def outer(weights_ref, pair):
        rows = hidden[2 * HID * pair : 2 * HID * (pair + 1)]
        return jnp.dot(weights_ref[...], rows, preferred_element_type=jnp.float32)

    both = outer(second_middle_ref, 1)
    half = 3 * PLANES // 2
    pairs = [both[:half] + outer(second_low_ref, 0), both[half:] + outer(second_high_ref, 2)]
    shift = lambda tap, by: pltpu.roll(tap, by, 1)
    part = PLANES // 2
    change = jnp.concatenate(
        [
            shift(p[:part], 1) + p[part : 2 * part] + shift(p[2 * part :], RING - 1)
            for p in pairs
        ],
        axis=0,
    )
    base = ring[2 * FIELDS : 2 * FIELDS + PLANES].astype(jnp.float32) + bias_ref[...]
    own = (base + change).astype(jnp.bfloat16)
    fields_ref[:, 0] = own[:, :LON].reshape(N_ENS, 8, LON)
    held_ref[pl.ds(pl.multiple_of(member * PLANES, PLANES), PLANES), :] = own

    count = observed_ref.shape[0]

    @pl.when(member == count - 1)
    def _():
        picked = jnp.dot(held_ref[...], column_ref[...], preferred_element_type=jnp.float32)
        here = lax.broadcasted_iota(jnp.int32, (PLANES, SLOTS), 0) == plane_ref[...]
        for m in range(count):
            mine = picked[m * PLANES : (m + 1) * PLANES]
            observed_ref[m : m + 1, :] = jnp.sum(
                jnp.where(here, mine, 0.0), axis=0, keepdims=True
            )


def cost(microseconds):
    return pl.CostEstimate(
        flops=int(microseconds * 1e9), transcendentals=0, bytes_accessed=int(microseconds * 1e6)
    )


def forecast(start, own, top, bottom, *shared):
    count = top.shape[0]
    whole = lambda array: pl.BlockSpec(array.shape, lambda m: (0,) * array.ndim)
    return pl.pallas_call(
        forecast_kernel,
        grid=(count,),
        in_specs=[
            pl.BlockSpec((1, ROWS, FIELDS, LON), lambda m: (start + m, 0, 0, 0)),
            pl.BlockSpec((1, 2, FIELDS, LON), lambda m: (m, 0, 0, 0)),
            pl.BlockSpec((1, 2, FIELDS, LON), lambda m: (m, 0, 0, 0)),
        ]
        + [whole(array) for array in shared],
        out_specs=[
            pl.BlockSpec((N_ENS, 1, 8, LON), lambda m: (0, m, 0, 0)),
            pl.BlockSpec((count, SLOTS), lambda m: (0, 0)),
        ],
        out_shape=[
            jax.ShapeDtypeStruct((N_ENS, count, 8, LON), jnp.bfloat16),
            jax.ShapeDtypeStruct((count, SLOTS), jnp.float32),
        ],
        scratch_shapes=[pltpu.VMEM((count * PLANES, RING), jnp.bfloat16)],
        cost_estimate=cost(2 * count),
        compiler_params=pltpu.CompilerParams(vmem_limit_bytes=VMEM_LIMIT),
    )(own, top, bottom, *shared)


def products_kernel(place_ref, count_ref, value_ref, sigma_ref, *refs):
    pieces, out_ref, held_ref = refs[:N_ENS], refs[N_ENS], refs[N_ENS + 1]
    for step, piece in enumerate(pieces):
        at = pl.multiple_of(place_ref[step] * GROUP, GROUP)
        held_ref[pl.ds(at, GROUP), :] = piece[...]
    observed = held_ref[...]
    mean = jnp.sum(observed, axis=0, keepdims=True) / MEMBERS
    slot = lax.broadcasted_iota(jnp.int32, (1, SLOTS), 1)
    live = (slot < count_ref[0]).astype(jnp.float32)
    sigma = sigma_ref[...]
    anomalies = (observed - mean) * (live / (sigma * math.sqrt(MEMBERS - 1)))
    innov = live * (value_ref[...] - mean) / sigma
    left = jnp.concatenate([anomalies, jnp.broadcast_to(innov, (8, SLOTS))], axis=0)
    out_ref[...] = lax.dot_general(
        left,
        anomalies,
        (((1,), (1,)), ((), ())),
        precision=lax.Precision.HIGHEST,
        preferred_element_type=jnp.float32,
    )


def products(pieces, places, count, value, sigma):
    vmem = pl.BlockSpec(memory_space=pltpu.VMEM)
    smem = pl.BlockSpec(memory_space=pltpu.SMEM)
    return pl.pallas_call(
        products_kernel,
        in_specs=[smem, smem] + [vmem] * (2 + N_ENS),
        out_specs=vmem,
        out_shape=jax.ShapeDtypeStruct((MEMBERS + 8, MEMBERS), jnp.float32),
        cost_estimate=cost(2),
        scratch_shapes=[pltpu.VMEM((MEMBERS, SLOTS), jnp.float32)],
    )(places, count, value.reshape(1, SLOTS), sigma.reshape(1, SLOTS), *pieces)


def transform_kernel(a_ref, b_ref, c_ref, d_ref, factor_ref, weights_ref, transform_ref):
    n = MEMBERS
    total = (a_ref[...] + b_ref[...]) + (c_ref[...] + d_ref[...])
    row = lax.broadcasted_iota(jnp.int32, (n, n), 0)
    column = lax.broadcasted_iota(jnp.int32, (n, n), 1)
    eye = (row == column).astype(jnp.float32)
    gram = total[0:n] + eye
    blocks = [[gram[b : b + 8], eye[b : b + 8]] for b in range(0, n, 8)]
    within = lax.broadcasted_iota(jnp.int32, (8, n), 0)
    wide = lambda value: jnp.broadcast_to(value, (8, n))
    for b in range(n // 8):
        upper, inverse = blocks[b]
        columns = [wide(upper[:, 8 * b + k : 8 * b + k + 1]) for k in range(8)]
        scales, steps, rows = [], [], []
        for k in range(8):
            scale = lax.rsqrt(wide(columns[k][k : k + 1]))
            share = columns[k] * scale
            step = {}
            for later in range(k + 1, 8):
                step[later] = wide(share[later : later + 1])
                columns[later] = columns[later] - share * step[later]
            upper_row = wide(upper[k : k + 1]) * scale
            inverse_row = wide(inverse[k : k + 1]) * scale
            share = jnp.where(within > k, share, 0.0)
            upper = jnp.where(within == k, upper_row, upper - share * upper_row)
            inverse = jnp.where(within == k, inverse_row, inverse - share * inverse_row)
            scales.append(scale)
            steps.append(step)
            rows.append((upper_row, inverse_row))
        for t in range(b + 1, n // 8):
            later_upper, later_inverse = blocks[t]
            columns = [wide(later_upper[:, 8 * b + k : 8 * b + k + 1]) for k in range(8)]
            for k in range(8):
                share = columns[k] * scales[k]
                for later in range(k + 1, 8):
                    columns[later] = columns[later] - share * steps[k][later]
                later_upper = later_upper - share * rows[k][0]
                later_inverse = later_inverse - share * rows[k][1]
            blocks[t] = [later_upper, later_inverse]
        blocks[b] = [upper, inverse]
    upper = jnp.concatenate([pair[0] for pair in blocks], axis=0)
    inverse = jnp.concatenate([pair[1] for pair in blocks], axis=0)
    factor_ref[...] = jnp.where(row <= column, upper, 0.0).T
    proj = total[n : n + 1]
    middle = jnp.sum(inverse * proj, axis=1, keepdims=True)
    weights = jnp.sum(inverse * middle, axis=0, keepdims=True) / math.sqrt(n - 1)
    weights_ref[...] = weights
    coeff = inverse + weights
    transform = coeff - jnp.mean(coeff, axis=1, keepdims=True) + 1.0 / n
    transform_ref[...] = transform.astype(jnp.bfloat16)


def transform_of(parts):
    vmem = pl.BlockSpec(memory_space=pltpu.VMEM)
    return pl.pallas_call(
        transform_kernel,
        in_specs=[vmem] * 4,
        out_specs=[vmem, vmem, vmem],
        out_shape=[
            jax.ShapeDtypeStruct((MEMBERS, MEMBERS), jnp.float32),
            jax.ShapeDtypeStruct((1, MEMBERS), jnp.float32),
            jax.ShapeDtypeStruct((MEMBERS, MEMBERS), jnp.bfloat16),
        ],
        cost_estimate=cost(12),
    )(*parts)


def update_kernel(transform_ref, early_ref, late_ref, out_ref, spread_ref):
    rows = MEMBERS * 8
    half = rows // 2

    @pl.when(pl.program_id(0) == 0)
    def _():
        shape = (rows, MEMBERS)
        row = lax.broadcasted_iota(jnp.int32, shape, 0)
        column = lax.broadcasted_iota(jnp.int32, shape, 1)
        held = row % half // 64 * GROUP + row // half * 8 + row % 64 // 8
        repeat = (row // 8 == column).astype(jnp.bfloat16)
        placed = (held == column).astype(jnp.bfloat16)
        tall = jnp.dot(repeat, transform_ref[...], preferred_element_type=jnp.float32)
        wide = lax.dot_general(
            tall.astype(jnp.bfloat16),
            placed,
            (((1,), (1,)), ((), ())),
            preferred_element_type=jnp.float32,
        )
        plane = lax.broadcasted_iota(jnp.int32, (rows, rows), 0) % 8
        same = plane == lax.broadcasted_iota(jnp.int32, (rows, rows), 1) % 8
        spread_ref[...] = jnp.where(same, wide, 0.0).astype(jnp.bfloat16)

    fields = jnp.concatenate([early_ref[...], late_ref[...]], axis=0)
    mixed = jnp.dot(spread_ref[...], fields, preferred_element_type=jnp.float32)
    out_ref[...] = mixed.astype(jnp.bfloat16)


def update(transform, early, late):
    rows = MEMBERS * 8
    half = pl.BlockSpec((rows // 2, 256), lambda k: (0, k))
    mixed = pl.pallas_call(
        update_kernel,
        grid=(RING // 256,),
        in_specs=[pl.BlockSpec((MEMBERS, MEMBERS), lambda k: (0, 0)), half, half],
        out_specs=pl.BlockSpec((rows, 256), lambda k: (0, k)),
        out_shape=jax.ShapeDtypeStruct((rows, LON), jnp.bfloat16),
        scratch_shapes=[pltpu.VMEM((rows, rows), jnp.bfloat16)],
        cost_estimate=cost(6),
        compiler_params=pltpu.CompilerParams(vmem_limit_bytes=VMEM_LIMIT),
    )(transform, early.reshape(rows // 2, LON), late.reshape(rows // 2, LON))
    return mixed.reshape(N_ENS, GROUP, 8, LON)


def first_weights(conv_in, bias_in, mask):
    kernel = conv_in.astype(jnp.float32) * 0.5
    by_tap = jnp.transpose(kernel, (0, 3, 2, 1))
    placed = [
        jnp.pad(by_tap, ((0, 0), (0, 0), (r, 2 - r), (0, 0))).reshape(HID, 15 * FIELDS)
        for r in range(3)
    ]
    half = bias_in * 0.5
    high = half.astype(jnp.bfloat16).astype(jnp.float32)
    middle = (half - high).astype(jnp.bfloat16).astype(jnp.float32)
    low = half - high - middle
    bias = jnp.pad(jnp.stack([high, middle, low], axis=1), ((0, 0), (0, 13)))
    rows = [jnp.concatenate([part, bias], axis=1) * mask[r] for r, part in enumerate(placed)]
    return jnp.concatenate(rows, axis=0).astype(jnp.bfloat16)


def second_weights(conv_out):
    by_tap = jnp.transpose(conv_out, (3, 0, 2, 1))
    placed = [jnp.pad(by_tap, ((0, 0), (0, 0), (r, 3 - r), (0, 0))) for r in range(ROWS)]
    whole = jnp.stack(placed, axis=1).reshape(3, 2, 2 * FIELDS, 6 * HID)
    low = whole[:, 0].reshape(6 * FIELDS, 6 * HID)
    high = whole[:, 1].reshape(6 * FIELDS, 6 * HID)
    pair = 2 * HID
    middle = jnp.concatenate([low[:, pair : 2 * pair], high[:, pair : 2 * pair]], axis=0)
    return low[:, :pair], middle, high[:, 2 * pair :]


def on_device(
    ensemble_weather,
    conv_in,
    bias_in,
    conv_out,
    bias_out,
    observed_entry_index,
    obs_count,
    obs_value,
    obs_sigma,
):
    tiles = lax.axis_size("map")
    tile = lax.axis_index("map")
    own_place = lax.axis_index("ens")
    down = [(i, i + 1) for i in range(tiles - 1)]
    up = [(i + 1, i) for i in range(tiles - 1)]

    def swap(value, axis, step):
        pairs = [(i, i ^ step) for i in range(lax.axis_size(axis))]
        return lax.ppermute(value, axis, pairs)

    own = jnp.transpose(ensemble_weather, (0, 2, 1, 3))
    share = GROUP // CHUNKS
    halos = []
    for chunk in range(CHUNKS):
        part = own[chunk * share : (chunk + 1) * share]
        edges = (part[:, ROWS - 2 :], part[:, :2])
        if halos:
            edges, halos[-1] = lax.optimization_barrier((edges, halos[-1]))
        halos.append((lax.ppermute(edges[0], "map", down), lax.ppermute(edges[1], "map", up)))
    one = jnp.float32(1.0)
    inner_top = (tile > 0).astype(jnp.float32)
    inner_bottom = (tile < tiles - 1).astype(jnp.float32)
    first_top = first_weights(conv_in, bias_in, [inner_top, one, one])
    first_bottom = first_weights(conv_in, bias_in, [one, one, inner_bottom])
    second_low, second_middle, second_high = second_weights(conv_out)
    bias = jnp.tile(bias_out, ROWS).reshape(PLANES, 1)
    plane = observed_entry_index // LON
    column = observed_entry_index - plane * LON
    picks = (jnp.arange(RING)[:, None] == column[None, :]).astype(jnp.bfloat16)
    plane = ((plane % ROWS) * FIELDS + plane // ROWS).reshape(1, SLOTS)

    exchange = lambda value: lax.all_to_all(
        value, "ens", split_axis=0, concat_axis=0, tiled=True
    )
    fields, observed = [], []
    for chunk, (top, bottom) in enumerate(halos):
        moved, seen = forecast(
            chunk * share,
            own,
            top,
            bottom,
            first_top,
            first_bottom,
            second_low,
            second_middle,
            second_high,
            bias,
            picks,
            plane,
        )
        fields.append(moved)
        observed.append(seen)
    early = exchange(fields[0])
    observed = jnp.concatenate(observed, axis=0)
    pieces = [observed] + [swap(observed, "ens", step) for step in range(1, N_ENS)]
    places = jnp.bitwise_xor(own_place, jnp.arange(N_ENS, dtype=jnp.int32))
    pieces, late = lax.optimization_barrier((pieces, fields[1]))
    late = exchange(late)
    part = products(pieces, places, obs_count, obs_value, obs_sigma)
    near = [part] + [swap(part, "map", step) for step in (1, 2, 3)]
    row = (near[0] + near[1]) + (near[2] + near[3])
    factor, mean_weights, transform = transform_of(
        [row] + [swap(row, "map", step) for step in (4, 8, 12)]
    )
    back = exchange(update(transform, early, late))
    back = back.reshape(ROWS, 2, GROUP, 8, LON)
    analysis = jnp.transpose(back, (2, 1, 3, 0, 4)).reshape(GROUP, FIELDS, ROWS, LON)
    return (analysis, factor, mean_weights.reshape(MEMBERS))


def solution(mesh):
    placed = (
        P("ens", None, "map", None),
        P(),
        P(),
        P(),
        P(),
        P("map"),
        P("map"),
        P("map"),
        P("map"),
    )
    return jax.shard_map(
        on_device,
        mesh=mesh,
        in_specs=placed,
        out_specs=(P("ens", None, "map", None), P(), P()),
        check_vma=False,
    )
```

```python
import functools
import math

import jax
import jax.numpy as jnp
from jax import lax
from jax.experimental import pallas as pl
from jax.experimental.pallas import tpu as pltpu
from jax.sharding import PartitionSpec as P

FIELDS = 16
HID = 128
ROWS = 4
LON = 1440
RING = 1536
SLOTS = 256
GROUP = 16
PLANES = ROWS * FIELDS
CHUNKS = 2
N_ENS = 8
MEMBERS = 128
VMEM_LIMIT = 56 * 1024 * 1024


def forecast_kernel(
    x_ref,
    top_ref,
    bottom_ref,
    first_top_ref,
    first_bottom_ref,
    second_low_ref,
    second_middle_ref,
    second_high_ref,
    bias_ref,
    column_ref,
    plane_ref,
    fields_ref,
    observed_ref,
    held_ref,
):
    member = pl.program_id(0)
    main = x_ref[0].reshape(PLANES, LON)
    stack = jnp.concatenate(
        [top_ref[0].reshape(2 * FIELDS, LON), main, bottom_ref[0].reshape(2 * FIELDS, LON)],
        axis=0,
    )
    ring = jnp.concatenate([stack, stack[:, :64], stack[:, LON - 32 :]], axis=1)
    left = pltpu.roll(ring, 1, 1)
    right = pltpu.roll(ring, RING - 1, 1)
    ones = jnp.ones((16, RING), jnp.bfloat16)

    def hidden_rows(low, weights_ref):
        high = low + 5 * FIELDS
        taps = jnp.concatenate([left[low:high], ring[low:high], right[low:high], ones], axis=0)
        half = jnp.dot(weights_ref[...], taps, preferred_element_type=jnp.float32)
        return (half * jnp.tanh(half) + half).astype(jnp.bfloat16)

    hidden = jnp.concatenate(
        [hidden_rows(0, first_top_ref), hidden_rows(3 * FIELDS, first_bottom_ref)], axis=0
    )

    def outer(weights_ref, pair):
        rows = hidden[2 * HID * pair : 2 * HID * (pair + 1)]
        return jnp.dot(weights_ref[...], rows, preferred_element_type=jnp.float32)

    both = outer(second_middle_ref, 1)
    half = 3 * PLANES // 2
    pairs = [both[:half] + outer(second_low_ref, 0), both[half:] + outer(second_high_ref, 2)]
    shift = lambda tap, by: pltpu.roll(tap, by, 1)
    part = PLANES // 2
    change = jnp.concatenate(
        [
            shift(p[:part], 1) + p[part : 2 * part] + shift(p[2 * part :], RING - 1)
            for p in pairs
        ],
        axis=0,
    )
    base = ring[2 * FIELDS : 2 * FIELDS + PLANES].astype(jnp.float32) + bias_ref[...]
    own = (base + change).astype(jnp.bfloat16)
    fields_ref[:, 0] = own[:, :LON].reshape(N_ENS, 8, LON)
    held_ref[pl.ds(pl.multiple_of(member * PLANES, PLANES), PLANES), :] = own

    count = observed_ref.shape[0]

    @pl.when(member == count - 1)
    def _():
        picked = jnp.dot(held_ref[...], column_ref[...], preferred_element_type=jnp.float32)
        here = lax.broadcasted_iota(jnp.int32, (PLANES, SLOTS), 0) == plane_ref[...]
        for m in range(count):
            mine = picked[m * PLANES : (m + 1) * PLANES]
            observed_ref[m : m + 1, :] = jnp.sum(
                jnp.where(here, mine, 0.0), axis=0, keepdims=True
            )


def cost(microseconds):
    return pl.CostEstimate(
        flops=int(microseconds * 1e9), transcendentals=0, bytes_accessed=int(microseconds * 1e6)
    )


def forecast(start, own, top, bottom, *shared):
    count = top.shape[0]
    whole = lambda array: pl.BlockSpec(array.shape, lambda m: (0,) * array.ndim)
    return pl.pallas_call(
        forecast_kernel,
        grid=(count,),
        in_specs=[
            pl.BlockSpec((1, ROWS, FIELDS, LON), lambda m: (start + m, 0, 0, 0)),
            pl.BlockSpec((1, 2, FIELDS, LON), lambda m: (m, 0, 0, 0)),
            pl.BlockSpec((1, 2, FIELDS, LON), lambda m: (m, 0, 0, 0)),
        ]
        + [whole(array) for array in shared],
        out_specs=[
            pl.BlockSpec((N_ENS, 1, 8, LON), lambda m: (0, m, 0, 0)),
            pl.BlockSpec((count, SLOTS), lambda m: (0, 0)),
        ],
        out_shape=[
            jax.ShapeDtypeStruct((N_ENS, count, 8, LON), jnp.bfloat16),
            jax.ShapeDtypeStruct((count, SLOTS), jnp.float32),
        ],
        scratch_shapes=[pltpu.VMEM((count * PLANES, RING), jnp.bfloat16)],
        cost_estimate=cost(2 * count),
        compiler_params=pltpu.CompilerParams(vmem_limit_bytes=VMEM_LIMIT),
    )(own, top, bottom, *shared)


def products_kernel(place_ref, count_ref, value_ref, sigma_ref, *refs):
    pieces, out_ref, held_ref = refs[:N_ENS], refs[N_ENS], refs[N_ENS + 1]
    for step, piece in enumerate(pieces):
        at = pl.multiple_of(place_ref[step] * GROUP, GROUP)
        held_ref[pl.ds(at, GROUP), :] = piece[...]
    observed = held_ref[...]
    mean = jnp.sum(observed, axis=0, keepdims=True) / MEMBERS
    slot = lax.broadcasted_iota(jnp.int32, (1, SLOTS), 1)
    live = (slot < count_ref[0]).astype(jnp.float32)
    sigma = sigma_ref[...]
    anomalies = (observed - mean) * (live / (sigma * math.sqrt(MEMBERS - 1)))
    innov = live * (value_ref[...] - mean) / sigma
    left = jnp.concatenate([anomalies, jnp.broadcast_to(innov, (8, SLOTS))], axis=0)
    out_ref[...] = lax.dot_general(
        left,
        anomalies,
        (((1,), (1,)), ((), ())),
        precision=lax.Precision.HIGHEST,
        preferred_element_type=jnp.float32,
    )


def products(pieces, places, count, value, sigma):
    vmem = pl.BlockSpec(memory_space=pltpu.VMEM)
    smem = pl.BlockSpec(memory_space=pltpu.SMEM)
    return pl.pallas_call(
        products_kernel,
        in_specs=[smem, smem] + [vmem] * (2 + N_ENS),
        out_specs=vmem,
        out_shape=jax.ShapeDtypeStruct((MEMBERS + 8, MEMBERS), jnp.float32),
        cost_estimate=cost(1),
        scratch_shapes=[pltpu.VMEM((MEMBERS, SLOTS), jnp.float32)],
    )(places, count, value.reshape(1, SLOTS), sigma.reshape(1, SLOTS), *pieces)


def transform_kernel(a_ref, b_ref, c_ref, d_ref, factor_ref, weights_ref, transform_ref):
    n = MEMBERS
    total = (a_ref[...] + b_ref[...]) + (c_ref[...] + d_ref[...])
    row = lax.broadcasted_iota(jnp.int32, (n, n), 0)
    column = lax.broadcasted_iota(jnp.int32, (n, n), 1)
    eye = (row == column).astype(jnp.float32)
    gram = total[0:n] + eye
    blocks = [[gram[b : b + 8], eye[b : b + 8]] for b in range(0, n, 8)]
    within = lax.broadcasted_iota(jnp.int32, (8, n), 0)
    wide = lambda value: jnp.broadcast_to(value, (8, n))
    for b in range(n // 8):
        upper, inverse = blocks[b]
        columns = [wide(upper[:, 8 * b + k : 8 * b + k + 1]) for k in range(8)]
        scales, steps, rows = [], [], []
        for k in range(8):
            scale = lax.rsqrt(wide(columns[k][k : k + 1]))
            share = columns[k] * scale
            step = {}
            for later in range(k + 1, 8):
                step[later] = wide(share[later : later + 1])
                columns[later] = columns[later] - share * step[later]
            upper_row = wide(upper[k : k + 1]) * scale
            inverse_row = wide(inverse[k : k + 1]) * scale
            share = jnp.where(within > k, share, 0.0)
            upper = jnp.where(within == k, upper_row, upper - share * upper_row)
            inverse = jnp.where(within == k, inverse_row, inverse - share * inverse_row)
            scales.append(scale)
            steps.append(step)
            rows.append((upper_row, inverse_row))
        for t in range(b + 1, n // 8):
            later_upper, later_inverse = blocks[t]
            columns = [wide(later_upper[:, 8 * b + k : 8 * b + k + 1]) for k in range(8)]
            for k in range(8):
                share = columns[k] * scales[k]
                for later in range(k + 1, 8):
                    columns[later] = columns[later] - share * steps[k][later]
                later_upper = later_upper - share * rows[k][0]
                later_inverse = later_inverse - share * rows[k][1]
            blocks[t] = [later_upper, later_inverse]
        blocks[b] = [upper, inverse]
    upper = jnp.concatenate([pair[0] for pair in blocks], axis=0)
    inverse = jnp.concatenate([pair[1] for pair in blocks], axis=0)
    factor_ref[...] = jnp.where(row <= column, upper, 0.0).T
    proj = total[n : n + 1]
    middle = jnp.sum(inverse * proj, axis=1, keepdims=True)
    weights = jnp.sum(inverse * middle, axis=0, keepdims=True) / math.sqrt(n - 1)
    weights_ref[...] = weights
    coeff = inverse + weights
    transform = coeff - jnp.mean(coeff, axis=1, keepdims=True) + 1.0 / n
    transform_ref[...] = transform.astype(jnp.bfloat16)


def transform_of(parts):
    vmem = pl.BlockSpec(memory_space=pltpu.VMEM)
    return pl.pallas_call(
        transform_kernel,
        in_specs=[vmem] * 4,
        out_specs=[vmem, vmem, vmem],
        out_shape=[
            jax.ShapeDtypeStruct((MEMBERS, MEMBERS), jnp.float32),
            jax.ShapeDtypeStruct((1, MEMBERS), jnp.float32),
            jax.ShapeDtypeStruct((MEMBERS, MEMBERS), jnp.bfloat16),
        ],
        cost_estimate=cost(1),
    )(*parts)


def update_kernel(transform_ref, early_ref, late_ref, out_ref, spread_ref):
    rows = MEMBERS * 8
    half = rows // 2

    @pl.when(pl.program_id(0) == 0)
    def _():
        shape = (rows, MEMBERS)
        row = lax.broadcasted_iota(jnp.int32, shape, 0)
        column = lax.broadcasted_iota(jnp.int32, shape, 1)
        held = row % half // 64 * GROUP + row // half * 8 + row % 64 // 8
        repeat = (row // 8 == column).astype(jnp.bfloat16)
        placed = (held == column).astype(jnp.bfloat16)
        tall = jnp.dot(repeat, transform_ref[...], preferred_element_type=jnp.float32)
        wide = lax.dot_general(
            tall.astype(jnp.bfloat16),
            placed,
            (((1,), (1,)), ((), ())),
            preferred_element_type=jnp.float32,
        )
        plane = lax.broadcasted_iota(jnp.int32, (rows, rows), 0) % 8
        same = plane == lax.broadcasted_iota(jnp.int32, (rows, rows), 1) % 8
        spread_ref[...] = jnp.where(same, wide, 0.0).astype(jnp.bfloat16)

    fields = jnp.concatenate([early_ref[...], late_ref[...]], axis=0)
    mixed = jnp.dot(spread_ref[...], fields, preferred_element_type=jnp.float32)
    out_ref[...] = mixed.astype(jnp.bfloat16)


def update(transform, early, late):
    rows = MEMBERS * 8
    half = pl.BlockSpec((rows // 2, 256), lambda k: (0, k))
    mixed = pl.pallas_call(
        update_kernel,
        grid=(RING // 256,),
        in_specs=[pl.BlockSpec((MEMBERS, MEMBERS), lambda k: (0, 0)), half, half],
        out_specs=pl.BlockSpec((rows, 256), lambda k: (0, k)),
        out_shape=jax.ShapeDtypeStruct((rows, LON), jnp.bfloat16),
        scratch_shapes=[pltpu.VMEM((rows, rows), jnp.bfloat16)],
        cost_estimate=cost(6),
        compiler_params=pltpu.CompilerParams(vmem_limit_bytes=VMEM_LIMIT),
    )(transform, early.reshape(rows // 2, LON), late.reshape(rows // 2, LON))
    return mixed.reshape(N_ENS, GROUP, 8, LON)


def first_weights(conv_in, bias_in, mask):
    kernel = conv_in.astype(jnp.float32) * 0.5
    by_tap = jnp.transpose(kernel, (0, 3, 2, 1))
    placed = [
        jnp.pad(by_tap, ((0, 0), (0, 0), (r, 2 - r), (0, 0))).reshape(HID, 15 * FIELDS)
        for r in range(3)
    ]
    half = bias_in * 0.5
    high = half.astype(jnp.bfloat16).astype(jnp.float32)
    middle = (half - high).astype(jnp.bfloat16).astype(jnp.float32)
    low = half - high - middle
    bias = jnp.pad(jnp.stack([high, middle, low], axis=1), ((0, 0), (0, 13)))
    rows = [jnp.concatenate([part, bias], axis=1) * mask[r] for r, part in enumerate(placed)]
    return jnp.concatenate(rows, axis=0).astype(jnp.bfloat16)


def second_weights(conv_out):
    by_tap = jnp.transpose(conv_out, (3, 0, 2, 1))
    placed = [jnp.pad(by_tap, ((0, 0), (0, 0), (r, 3 - r), (0, 0))) for r in range(ROWS)]
    whole = jnp.stack(placed, axis=1).reshape(3, 2, 2 * FIELDS, 6 * HID)
    low = whole[:, 0].reshape(6 * FIELDS, 6 * HID)
    high = whole[:, 1].reshape(6 * FIELDS, 6 * HID)
    pair = 2 * HID
    middle = jnp.concatenate([low[:, pair : 2 * pair], high[:, pair : 2 * pair]], axis=0)
    return low[:, :pair], middle, high[:, 2 * pair :]


def on_device(
    ensemble_weather,
    conv_in,
    bias_in,
    conv_out,
    bias_out,
    observed_entry_index,
    obs_count,
    obs_value,
    obs_sigma,
):
    tiles = lax.axis_size("map")
    tile = lax.axis_index("map")
    own_place = lax.axis_index("ens")
    down = [(i, i + 1) for i in range(tiles - 1)]
    up = [(i + 1, i) for i in range(tiles - 1)]

    def swap(value, axis, step):
        pairs = [(i, i ^ step) for i in range(lax.axis_size(axis))]
        return lax.ppermute(value, axis, pairs)

    share = GROUP // CHUNKS

    def edges(chunk):
        part = ensemble_weather[chunk * share : (chunk + 1) * share]
        rows = lambda low: jnp.transpose(part[:, :, low : low + 2], (0, 2, 1, 3))
        return rows(ROWS - 2), rows(0)

    def halo(rows):
        return lax.ppermute(rows[0], "map", down), lax.ppermute(rows[1], "map", up)

    own_edges = edges(0)
    halos = [halo(own_edges)]
    own_edges, ensemble_weather = lax.optimization_barrier((own_edges, ensemble_weather))
    own = jnp.transpose(ensemble_weather, (0, 2, 1, 3))
    one = jnp.float32(1.0)
    inner_top = (tile > 0).astype(jnp.float32)
    inner_bottom = (tile < tiles - 1).astype(jnp.float32)
    first_top = first_weights(conv_in, bias_in, [inner_top, one, one])
    first_bottom = first_weights(conv_in, bias_in, [one, one, inner_bottom])
    second_low, second_middle, second_high = second_weights(conv_out)
    bias = jnp.tile(bias_out, ROWS).reshape(PLANES, 1)
    plane = observed_entry_index // LON
    column = observed_entry_index - plane * LON
    picks = (jnp.arange(RING)[:, None] == column[None, :]).astype(jnp.bfloat16)
    plane = ((plane % ROWS) * FIELDS + plane // ROWS).reshape(1, SLOTS)
    exchange = lambda value: lax.all_to_all(
        value, "ens", split_axis=0, concat_axis=0, tiled=True
    )
    next_edges, picks = lax.optimization_barrier((edges(1), picks))
    halos.append(halo(next_edges))

    fields, observed = [], []
    for chunk, (top, bottom) in enumerate(halos):
        moved, seen = forecast(
            chunk * share,
            own,
            top,
            bottom,
            first_top,
            first_bottom,
            second_low,
            second_middle,
            second_high,
            bias,
            picks,
            plane,
        )
        fields.append(moved)
        observed.append(seen)
    early = exchange(fields[0])
    observed = jnp.concatenate(observed, axis=0)
    pieces = [observed] + [swap(observed, "ens", step) for step in range(1, N_ENS)]
    places = jnp.bitwise_xor(own_place, jnp.arange(N_ENS, dtype=jnp.int32))
    pieces, late, early = lax.optimization_barrier((pieces, fields[1], early))
    late = exchange(late)
    part = products(pieces, places, obs_count, obs_value, obs_sigma)
    near = [part] + [swap(part, "map", step) for step in (1, 2, 3)]
    row = (near[0] + near[1]) + (near[2] + near[3])
    factor, mean_weights, transform = transform_of(
        [row] + [swap(row, "map", step) for step in (4, 8, 12)]
    )
    back = exchange(update(transform, early, late))
    back = back.reshape(ROWS, 2, GROUP, 8, LON)
    analysis = jnp.transpose(back, (2, 1, 3, 0, 4)).reshape(GROUP, FIELDS, ROWS, LON)
    return (analysis, factor, mean_weights.reshape(MEMBERS))


def solution(mesh):
    placed = (
        P("ens", None, "map", None),
        P(),
        P(),
        P(),
        P(),
        P("map"),
        P("map"),
        P("map"),
        P("map"),
    )
    return jax.shard_map(
        on_device,
        mesh=mesh,
        in_specs=placed,
        out_specs=(P("ens", None, "map", None), P(), P()),
        check_vma=False,
    )
```

```python
import functools
import math

import jax
import jax.numpy as jnp
from jax import lax
from jax.experimental import pallas as pl
from jax.experimental.pallas import tpu as pltpu
from jax.sharding import PartitionSpec as P

FIELDS = 16
HID = 128
ROWS = 4
LON = 1440
RING = 1536
SLOTS = 256
GROUP = 16
PLANES = ROWS * FIELDS
CHUNKS = 2
STEP = 4
N_ENS = 8
MEMBERS = 128
VMEM_LIMIT = 56 * 1024 * 1024


def prepare_kernel(
    tile_ref,
    first_ref,
    bias_in_ref,
    second_ref,
    bias_out_ref,
    index_ref,
    top_ref,
    bottom_ref,
    low_ref,
    middle_ref,
    high_ref,
    bias_ref,
    picks_ref,
    plane_ref,
    *,
    tiles,
):
    tap = lambda ref, row, column: ref[(3 * row + column) * 16 : (3 * row + column + 1) * 16]
    half = bias_in_ref[...] * 0.5
    high = half.astype(jnp.bfloat16).astype(jnp.float32)
    middle = (half - high).astype(jnp.bfloat16).astype(jnp.float32)
    low = half - high - middle
    zeros = jnp.zeros((16, HID), jnp.float32)
    bias = jnp.concatenate([high, middle, low, zeros[:13]], axis=0)
    parts = []
    for r in range(3):
        pieces = []
        for column in range(3):
            for row in range(5):
                known = 0 <= row - r <= 2
                piece = tap(first_ref, row - r, column).astype(jnp.float32) if known else zeros
                pieces.append(piece * 0.5)
        parts.append(jnp.concatenate(pieces + [bias], axis=0).T)
    tile = tile_ref[0]
    inner_top = jnp.where(tile > 0, 1.0, 0.0)
    inner_bottom = jnp.where(tile < tiles - 1, 1.0, 0.0)
    top = jnp.concatenate([parts[0] * inner_top, parts[1], parts[2]], axis=0)
    bottom = jnp.concatenate([parts[0], parts[1], parts[2] * inner_bottom], axis=0)
    top_ref[...] = top.astype(jnp.bfloat16)
    bottom_ref[...] = bottom.astype(jnp.bfloat16)

    rows = 6 * FIELDS
    to = lax.broadcasted_iota(jnp.int32, (rows, rows), 0)
    source = to // 32 * 32 + to % 2 * 16 + to % 32 // 2
    turn = (source == lax.broadcasted_iota(jnp.int32, (rows, rows), 1)).astype(jnp.bfloat16)

    def placed(taps):
        blank = jnp.zeros((16, HID), jnp.bfloat16)
        lines = []
        for column in range(3):
            for line in taps:
                cells = [blank if d is None else tap(second_ref, d, column) for d in line]
                lines.append(jnp.concatenate(cells, axis=1))
        whole = jnp.concatenate(lines, axis=0)
        return jnp.dot(turn, whole, preferred_element_type=jnp.float32).astype(jnp.bfloat16)

    upper = placed(((0, 1), (None, 0)))
    lower = placed(((2, None), (1, 2)))
    low_ref[...] = upper
    middle_ref[...] = jnp.concatenate([lower, upper], axis=0)
    high_ref[...] = lower

    group = 16 * FIELDS
    field = lax.broadcasted_iota(jnp.int32, (group, FIELDS), 0) // 16
    mine = field == lax.broadcasted_iota(jnp.int32, (group, FIELDS), 1)
    bias_ref[...] = jnp.sum(jnp.where(mine, bias_out_ref[...], 0.0), axis=1, keepdims=True)

    entry = index_ref[...]
    bound = (lax.broadcasted_iota(jnp.int32, (PLANES, SLOTS), 0) + 1) * LON
    plane = jnp.sum(jnp.where(entry >= bound, 1, 0), axis=0, keepdims=True)
    plane_ref[...] = plane
    column = entry - plane * LON
    for at in range(0, RING, 256):
        place = lax.broadcasted_iota(jnp.int32, (256, SLOTS), 0) + at
        picks_ref[at : at + 256, :] = jnp.where(place == column, 1.0, 0.0).astype(jnp.bfloat16)


def prepare(tile, tiles, conv_in, bias_in, conv_out, bias_out, index):
    vmem = pl.BlockSpec(memory_space=pltpu.VMEM)
    shape = jax.ShapeDtypeStruct
    return pl.pallas_call(
        functools.partial(prepare_kernel, tiles=tiles),
        in_specs=[pl.BlockSpec(memory_space=pltpu.SMEM)] + [vmem] * 5,
        out_specs=[vmem] * 8,
        out_shape=[
            shape((3 * HID, 256), jnp.bfloat16),
            shape((3 * HID, 256), jnp.bfloat16),
            shape((6 * FIELDS, 2 * HID), jnp.bfloat16),
            shape((12 * FIELDS, 2 * HID), jnp.bfloat16),
            shape((6 * FIELDS, 2 * HID), jnp.bfloat16),
            shape((16 * FIELDS, 1), jnp.float32),
            shape((RING, SLOTS), jnp.bfloat16),
            shape((1, SLOTS), jnp.int32),
        ],
        cost_estimate=cost(3),
    )(
        tile.astype(jnp.int32).reshape(1),
        jnp.transpose(conv_in, (2, 3, 1, 0)).reshape(9 * FIELDS, HID),
        bias_in.reshape(1, HID),
        jnp.transpose(conv_out, (2, 3, 0, 1)).reshape(9 * FIELDS, HID),
        bias_out.reshape(1, FIELDS),
        index.reshape(1, SLOTS),
    )


def forecast_kernel(
    x_ref,
    base_ref,
    top_ref,
    bottom_ref,
    first_top_ref,
    first_bottom_ref,
    low_ref,
    middle_ref,
    high_ref,
    bias_ref,
    picks_ref,
    plane_ref,
    earlier_ref,
    fields_ref,
    observed_ref,
    held_ref,
):
    step = pl.program_id(0)
    ones = jnp.ones((16, RING), jnp.bfloat16)
    part = PLANES // 2

    def changes(member):
        stack = jnp.concatenate(
            [
                top_ref[member].reshape(2 * FIELDS, LON),
                x_ref[member].reshape(PLANES, LON),
                bottom_ref[member].reshape(2 * FIELDS, LON),
            ],
            axis=0,
        )
        ring = jnp.concatenate([stack, stack[:, :64], stack[:, LON - 32 :]], axis=1)
        left = pltpu.roll(ring, 1, 1)
        right = pltpu.roll(ring, RING - 1, 1)

        def hidden_rows(at, weights_ref):
            to = at + 5 * FIELDS
            taps = jnp.concatenate([left[at:to], ring[at:to], right[at:to], ones], axis=0)
            half = jnp.dot(weights_ref[...], taps, preferred_element_type=jnp.float32)
            return (half * jnp.tanh(half) + half).astype(jnp.bfloat16)

        hidden = jnp.concatenate(
            [hidden_rows(0, first_top_ref), hidden_rows(3 * FIELDS, first_bottom_ref)], axis=0
        )

        def outer(weights_ref, pair):
            rows = hidden[2 * HID * pair : 2 * HID * (pair + 1)]
            return jnp.dot(weights_ref[...], rows, preferred_element_type=jnp.float32)

        both = outer(middle_ref, 1)
        for taps in (both[: 3 * part] + outer(low_ref, 0), both[3 * part :] + outer(high_ref, 2)):
            yield (
                pltpu.roll(taps[:part], 1, 1)
                + taps[part : 2 * part]
                + pltpu.roll(taps[2 * part :], RING - 1, 1)
            )

    sub = lax.broadcasted_iota(jnp.int32, (8, RING), 0)
    pairs = []
    for pair in range(STEP // 2):
        sources = [*changes(2 * pair), *changes(2 * pair + 1)]
        blocks = []
        for field in range(FIELDS):
            at, by = field // 4 * 8, field % 4 * 2
            moved = [
                pltpu.roll(source[at : at + 8], (2 * k - by) % 8, 0) if (2 * k - by) % 8 else source[at : at + 8]
                for k, source in enumerate(sources)
            ]
            first = jnp.where(sub < 2, moved[0], moved[1])
            last = jnp.where(sub < 6, moved[2], moved[3])
            blocks.append(jnp.where(sub < 4, first, last))
        pairs.append(blocks)
    for field in range(FIELDS):
        low, high = field * 16, field * 16 + 16
        base = base_ref[0, low:high, :].astype(jnp.float32) + bias_ref[low:high, :]
        base = jnp.concatenate([base, base[:, : RING - LON]], axis=1)
        change = jnp.concatenate([blocks[field] for blocks in pairs], axis=0)
        own = (base + change).astype(jnp.bfloat16)
        fields_ref[field // 2, field % 2] = own[:, :LON]
        held_ref[pl.ds(pl.multiple_of(step * 16 * FIELDS + low, 16), 16), :] = own

    @pl.when(step == pl.num_programs(0) - 1)
    def _():
        rows = held_ref.shape[0]
        picked = jnp.dot(held_ref[...], picks_ref[...], preferred_element_type=jnp.float32)
        row = lax.broadcasted_iota(jnp.int32, (rows, SLOTS), 0)
        here = row % 256 // 16 * ROWS + row % ROWS == plane_ref[...]
        found = jnp.where(here, picked, 0.0).astype(jnp.bfloat16)
        count = rows // PLANES
        column = lax.broadcasted_iota(jnp.int32, (count, rows), 1)
        member = column // 256 * STEP + column % 16 // ROWS
        mine = member == lax.broadcasted_iota(jnp.int32, (count, rows), 0)
        seen = jnp.dot(
            mine.astype(jnp.bfloat16), found, preferred_element_type=jnp.float32
        )
        if earlier_ref is not None:
            seen = jnp.concatenate([earlier_ref[...], seen], axis=0)
        observed_ref[...] = seen


def cost(microseconds):
    return pl.CostEstimate(
        flops=int(microseconds * 1e9), transcendentals=0, bytes_accessed=int(microseconds * 1e6)
    )


def forecast(start, own, base, top, bottom, shared, earlier):
    count = top.shape[0]
    steps = count // STEP
    first = start // STEP
    whole = lambda array: pl.BlockSpec(array.shape, lambda m: (0,) * array.ndim)
    kernel = forecast_kernel
    if earlier is None:
        kernel = lambda *refs: forecast_kernel(*refs[:-3], None, *refs[-3:])
        seen = count
    else:
        shared = [*shared, earlier]
        seen = count + earlier.shape[0]
    return pl.pallas_call(
        kernel,
        grid=(steps,),
        in_specs=[
            pl.BlockSpec((STEP, ROWS, FIELDS, LON), lambda m: (first + m, 0, 0, 0)),
            pl.BlockSpec((1, 16 * FIELDS, LON), lambda m: (first + m, 0, 0)),
            pl.BlockSpec((STEP, 2, FIELDS, LON), lambda m: (m, 0, 0, 0)),
            pl.BlockSpec((STEP, 2, FIELDS, LON), lambda m: (m, 0, 0, 0)),
        ]
        + [whole(array) for array in shared],
        out_specs=[
            pl.BlockSpec((N_ENS, 2, 16, LON), lambda m: (0, 0, m, 0)),
            pl.BlockSpec((seen, SLOTS), lambda m: (0, 0)),
        ],
        out_shape=[
            jax.ShapeDtypeStruct((N_ENS, 2, count * ROWS, LON), jnp.bfloat16),
            jax.ShapeDtypeStruct((seen, SLOTS), jnp.float32),
        ],
        scratch_shapes=[pltpu.VMEM((count * PLANES, RING), jnp.bfloat16)],
        cost_estimate=cost(2 * count),
        compiler_params=pltpu.CompilerParams(vmem_limit_bytes=VMEM_LIMIT),
    )(own, base, top, bottom, *shared)


def products_kernel(place_ref, count_ref, value_ref, sigma_ref, *refs):
    pieces, out_ref, held_ref = refs[:N_ENS], refs[N_ENS], refs[N_ENS + 1]
    for step, piece in enumerate(pieces):
        at = pl.multiple_of((place_ref[0] ^ step) * GROUP, GROUP)
        held_ref[pl.ds(at, GROUP), :] = piece[...]
    observed = held_ref[...]
    mean = jnp.sum(observed, axis=0, keepdims=True) / MEMBERS
    slot = lax.broadcasted_iota(jnp.int32, (1, SLOTS), 1)
    live = (slot < count_ref[0]).astype(jnp.float32)
    sigma = sigma_ref[...]
    anomalies = (observed - mean) * (live / (sigma * math.sqrt(MEMBERS - 1)))
    innov = live * (value_ref[...] - mean) / sigma
    left = jnp.concatenate([anomalies, jnp.broadcast_to(innov, (8, SLOTS))], axis=0)
    out_ref[...] = lax.dot_general(
        left,
        anomalies,
        (((1,), (1,)), ((), ())),
        precision=lax.Precision.HIGHEST,
        preferred_element_type=jnp.float32,
    )


def products(pieces, places, count, value, sigma):
    vmem = pl.BlockSpec(memory_space=pltpu.VMEM)
    smem = pl.BlockSpec(memory_space=pltpu.SMEM)
    return pl.pallas_call(
        products_kernel,
        in_specs=[smem, smem] + [vmem] * (2 + N_ENS),
        out_specs=vmem,
        out_shape=jax.ShapeDtypeStruct((MEMBERS + 8, MEMBERS), jnp.float32),
        cost_estimate=cost(1),
        scratch_shapes=[pltpu.VMEM((MEMBERS, SLOTS), jnp.float32)],
    )(places, count, value.reshape(1, SLOTS), sigma.reshape(1, SLOTS), *pieces)


def transform_kernel(a_ref, b_ref, c_ref, d_ref, factor_ref, weights_ref, transform_ref):
    n = MEMBERS
    total = (a_ref[...] + b_ref[...]) + (c_ref[...] + d_ref[...])
    row = lax.broadcasted_iota(jnp.int32, (n, n), 0)
    column = lax.broadcasted_iota(jnp.int32, (n, n), 1)
    eye = (row == column).astype(jnp.float32)
    gram = total[0:n] + eye
    blocks = [[gram[b : b + 8], eye[b : b + 8]] for b in range(0, n, 8)]
    within = lax.broadcasted_iota(jnp.int32, (8, n), 0)
    wide = lambda value: jnp.broadcast_to(value, (8, n))
    for b in range(n // 8):
        upper, inverse = blocks[b]
        columns = [wide(upper[:, 8 * b + k : 8 * b + k + 1]) for k in range(8)]
        scales, steps, rows = [], [], []
        for k in range(8):
            scale = lax.rsqrt(wide(columns[k][k : k + 1]))
            share = columns[k] * scale
            step = {}
            for later in range(k + 1, 8):
                step[later] = wide(share[later : later + 1])
                columns[later] = columns[later] - share * step[later]
            upper_row = wide(upper[k : k + 1]) * scale
            inverse_row = wide(inverse[k : k + 1]) * scale
            share = jnp.where(within > k, share, 0.0)
            upper = jnp.where(within == k, upper_row, upper - share * upper_row)
            inverse = jnp.where(within == k, inverse_row, inverse - share * inverse_row)
            scales.append(scale)
            steps.append(step)
            rows.append((upper_row, inverse_row))
        for t in range(b + 1, n // 8):
            later_upper, later_inverse = blocks[t]
            columns = [wide(later_upper[:, 8 * b + k : 8 * b + k + 1]) for k in range(8)]
            for k in range(8):
                share = columns[k] * scales[k]
                for later in range(k + 1, 8):
                    columns[later] = columns[later] - share * steps[k][later]
                later_upper = later_upper - share * rows[k][0]
                later_inverse = later_inverse - share * rows[k][1]
            blocks[t] = [later_upper, later_inverse]
        blocks[b] = [upper, inverse]
    upper = jnp.concatenate([pair[0] for pair in blocks], axis=0)
    inverse = jnp.concatenate([pair[1] for pair in blocks], axis=0)
    factor_ref[...] = jnp.where(row <= column, upper, 0.0).T
    proj = total[n : n + 1]
    middle = jnp.sum(inverse * proj, axis=1, keepdims=True)
    weights = jnp.sum(inverse * middle, axis=0, keepdims=True) / math.sqrt(n - 1)
    weights_ref[...] = weights
    coeff = inverse + weights
    transform = coeff - jnp.mean(coeff, axis=1, keepdims=True) + 1.0 / n
    transform_ref[...] = transform.astype(jnp.bfloat16)


def transform_of(parts):
    vmem = pl.BlockSpec(memory_space=pltpu.VMEM)
    return pl.pallas_call(
        transform_kernel,
        in_specs=[vmem] * 4,
        out_specs=[vmem, vmem, vmem],
        out_shape=[
            jax.ShapeDtypeStruct((MEMBERS, MEMBERS), jnp.float32),
            jax.ShapeDtypeStruct((1, MEMBERS), jnp.float32),
            jax.ShapeDtypeStruct((MEMBERS, MEMBERS), jnp.bfloat16),
        ],
        cost_estimate=cost(1),
    )(*parts)


def update_kernel(transform_ref, early_ref, late_ref, out_ref, spread_ref):
    rows = MEMBERS * ROWS
    half = rows // 2

    @pl.when((pl.program_id(0) == 0) & (pl.program_id(1) == 0))
    def _():
        shape = (rows, MEMBERS)
        row = lax.broadcasted_iota(jnp.int32, shape, 0)
        column = lax.broadcasted_iota(jnp.int32, shape, 1)
        held = row % half // 32 * GROUP + row // half * 8 + row % 32 // ROWS
        repeat = (row // ROWS == column).astype(jnp.bfloat16)
        placed = (held == column).astype(jnp.bfloat16)
        tall = jnp.dot(repeat, transform_ref[...], preferred_element_type=jnp.float32)
        wide = lax.dot_general(
            tall.astype(jnp.bfloat16),
            placed,
            (((1,), (1,)), ((), ())),
            preferred_element_type=jnp.float32,
        )
        own = lax.broadcasted_iota(jnp.int32, (rows, rows), 0) % ROWS
        same = own == lax.broadcasted_iota(jnp.int32, (rows, rows), 1) % ROWS
        spread_ref[...] = jnp.where(same, wide, 0.0).astype(jnp.bfloat16)

    width = early_ref.shape[-1]
    fields = jnp.concatenate(
        [early_ref[:, 0].reshape(half, width), late_ref[:, 0].reshape(half, width)], axis=0
    )
    mixed = jnp.dot(spread_ref[...], fields, preferred_element_type=jnp.float32)
    out_ref[:, 0] = mixed.astype(jnp.bfloat16).reshape(N_ENS, GROUP * ROWS, width)


def update(transform, early, late):
    rows = MEMBERS * ROWS
    half = pl.BlockSpec((N_ENS, 1, 8 * ROWS, RING // 2), lambda c, x: (0, c, 0, x))
    return pl.pallas_call(
        update_kernel,
        grid=(2, 2),
        in_specs=[pl.BlockSpec((MEMBERS, MEMBERS), lambda c, x: (0, 0)), half, half],
        out_specs=pl.BlockSpec(
            (N_ENS, 1, GROUP * ROWS, RING // 2), lambda c, x: (0, c, 0, x)
        ),
        out_shape=jax.ShapeDtypeStruct((N_ENS, 2, GROUP * ROWS, LON), jnp.bfloat16),
        scratch_shapes=[pltpu.VMEM((rows, rows), jnp.bfloat16)],
        cost_estimate=cost(4),
        compiler_params=pltpu.CompilerParams(vmem_limit_bytes=VMEM_LIMIT),
    )(transform, early, late)


def on_device(
    ensemble_weather,
    conv_in,
    bias_in,
    conv_out,
    bias_out,
    observed_entry_index,
    obs_count,
    obs_value,
    obs_sigma,
):
    tiles = lax.axis_size("map")
    tile = lax.axis_index("map")
    own_place = lax.axis_index("ens")
    down = [(i, i + 1) for i in range(tiles - 1)]
    up = [(i + 1, i) for i in range(tiles - 1)]

    def swap(value, axis, step):
        pairs = [(i, i ^ step) for i in range(lax.axis_size(axis))]
        return lax.ppermute(value, axis, pairs)

    share = GROUP // CHUNKS
    exchange = lambda value: lax.all_to_all(
        value, "ens", split_axis=0, concat_axis=0, tiled=True
    )
    own = jnp.transpose(ensemble_weather, (0, 2, 1, 3))

    def edges(chunk):
        part = own[chunk * share : (chunk + 1) * share]
        return part[:, ROWS - 2 :], part[:, :2]

    def halo(rows):
        return lax.ppermute(rows[0], "map", down), lax.ppermute(rows[1], "map", up)

    halos = [halo(edges(0))]
    shared = prepare(
        tile, tiles, conv_in, bias_in, conv_out, bias_out, observed_entry_index
    )
    next_edges, shared = lax.optimization_barrier((edges(1), shared))
    halos.append(halo(next_edges))
    base = jnp.transpose(
        ensemble_weather.reshape(GROUP // STEP, STEP, FIELDS, ROWS, LON), (0, 2, 1, 3, 4)
    ).reshape(GROUP // STEP, STEP * PLANES, LON)
    fields, observed = [], None
    for chunk, (top, bottom) in enumerate(halos):
        moved, observed = forecast(chunk * share, own, base, top, bottom, shared, observed)
        fields.append(moved)
    early = exchange(fields[0])
    pieces = [observed] + [swap(observed, "ens", step) for step in range(1, N_ENS)]
    places = own_place.astype(jnp.int32).reshape(1)
    pieces, late, early = lax.optimization_barrier((pieces, fields[1], early))
    late = exchange(late)
    part = products(pieces, places, obs_count, obs_value, obs_sigma)
    near = [part] + [swap(part, "map", step) for step in (1, 2, 3)]
    row = (near[0] + near[1]) + (near[2] + near[3])
    factor, mean_weights, transform = transform_of(
        [row] + [swap(row, "map", step) for step in (4, 8, 12)]
    )
    back = exchange(update(transform, early, late))
    back = back.reshape(N_ENS, 2, GROUP, ROWS, LON)
    analysis = jnp.transpose(back, (2, 0, 1, 3, 4)).reshape(GROUP, FIELDS, ROWS, LON)
    return (analysis, factor, mean_weights.reshape(MEMBERS))


def solution(mesh):
    placed = (
        P("ens", None, "map", None),
        P(),
        P(),
        P(),
        P(),
        P("map"),
        P("map"),
        P("map"),
        P("map"),
    )
    return jax.shard_map(
        on_device,
        mesh=mesh,
        in_specs=placed,
        out_specs=(P("ens", None, "map", None), P(), P()),
        check_vma=False,
    )
```

```python
import functools
import math

import jax
import jax.numpy as jnp
from jax import lax
from jax.experimental import pallas as pl
from jax.experimental.pallas import tpu as pltpu
from jax.sharding import PartitionSpec as P

FIELDS = 16
HID = 128
ROWS = 4
LON = 1440
RING = 1536
SLOTS = 256
GROUP = 16
PLANES = ROWS * FIELDS
CHUNKS = 2
STEP = 4
N_ENS = 8
MEMBERS = 128
VMEM_LIMIT = 56 * 1024 * 1024


def prepare_kernel(
    tile_ref,
    first_ref,
    bias_in_ref,
    second_ref,
    bias_out_ref,
    index_ref,
    top_ref,
    bottom_ref,
    low_ref,
    middle_ref,
    high_ref,
    bias_ref,
    picks_ref,
    plane_ref,
    *,
    tiles,
):
    tap = lambda ref, row, column: ref[(3 * row + column) * 16 : (3 * row + column + 1) * 16]
    half = bias_in_ref[...] * 0.5
    high = half.astype(jnp.bfloat16).astype(jnp.float32)
    middle = (half - high).astype(jnp.bfloat16).astype(jnp.float32)
    low = half - high - middle
    zeros = jnp.zeros((16, HID), jnp.float32)
    bias = jnp.concatenate([high, middle, low, zeros[:13]], axis=0)
    parts = []
    for r in range(3):
        pieces = []
        for column in range(3):
            for row in range(5):
                known = 0 <= row - r <= 2
                piece = tap(first_ref, row - r, column).astype(jnp.float32) if known else zeros
                pieces.append(piece * 0.5)
        parts.append(jnp.concatenate(pieces + [bias], axis=0).T)
    tile = tile_ref[0]
    inner_top = jnp.where(tile > 0, 1.0, 0.0)
    inner_bottom = jnp.where(tile < tiles - 1, 1.0, 0.0)
    top = jnp.concatenate([parts[0] * inner_top, parts[1], parts[2]], axis=0)
    bottom = jnp.concatenate([parts[0], parts[1], parts[2] * inner_bottom], axis=0)
    top_ref[...] = top.astype(jnp.bfloat16)
    bottom_ref[...] = bottom.astype(jnp.bfloat16)

    rows = 6 * FIELDS
    to = lax.broadcasted_iota(jnp.int32, (rows, rows), 0)
    source = to // 32 * 32 + to % 2 * 16 + to % 32 // 2
    turn = (source == lax.broadcasted_iota(jnp.int32, (rows, rows), 1)).astype(jnp.bfloat16)

    def placed(taps):
        blank = jnp.zeros((16, HID), jnp.bfloat16)
        lines = []
        for column in range(3):
            for line in taps:
                cells = [blank if d is None else tap(second_ref, d, column) for d in line]
                lines.append(jnp.concatenate(cells, axis=1))
        whole = jnp.concatenate(lines, axis=0)
        return jnp.dot(turn, whole, preferred_element_type=jnp.float32).astype(jnp.bfloat16)

    upper = placed(((0, 1), (None, 0)))
    lower = placed(((2, None), (1, 2)))
    low_ref[...] = upper
    middle_ref[...] = jnp.concatenate([lower, upper], axis=0)
    high_ref[...] = lower

    group = 16 * FIELDS
    field = lax.broadcasted_iota(jnp.int32, (group, FIELDS), 0) // 16
    mine = field == lax.broadcasted_iota(jnp.int32, (group, FIELDS), 1)
    bias_ref[...] = jnp.sum(jnp.where(mine, bias_out_ref[...], 0.0), axis=1, keepdims=True)

    entry = index_ref[...]
    bound = (lax.broadcasted_iota(jnp.int32, (PLANES, SLOTS), 0) + 1) * LON
    plane = jnp.sum(jnp.where(entry >= bound, 1, 0), axis=0, keepdims=True)
    plane_ref[...] = plane
    column = entry - plane * LON
    for at in range(0, RING, 256):
        place = lax.broadcasted_iota(jnp.int32, (256, SLOTS), 0) + at
        picks_ref[at : at + 256, :] = jnp.where(place == column, 1.0, 0.0).astype(jnp.bfloat16)


def prepare(tile, tiles, conv_in, bias_in, conv_out, bias_out, index):
    vmem = pl.BlockSpec(memory_space=pltpu.VMEM)
    shape = jax.ShapeDtypeStruct
    return pl.pallas_call(
        functools.partial(prepare_kernel, tiles=tiles),
        in_specs=[pl.BlockSpec(memory_space=pltpu.SMEM)] + [vmem] * 5,
        out_specs=[vmem] * 8,
        out_shape=[
            shape((3 * HID, 256), jnp.bfloat16),
            shape((3 * HID, 256), jnp.bfloat16),
            shape((6 * FIELDS, 2 * HID), jnp.bfloat16),
            shape((12 * FIELDS, 2 * HID), jnp.bfloat16),
            shape((6 * FIELDS, 2 * HID), jnp.bfloat16),
            shape((16 * FIELDS, 1), jnp.float32),
            shape((RING, SLOTS), jnp.bfloat16),
            shape((1, SLOTS), jnp.int32),
        ],
        cost_estimate=cost(3),
    )(
        tile.astype(jnp.int32).reshape(1),
        jnp.transpose(conv_in, (2, 3, 1, 0)).reshape(9 * FIELDS, HID),
        bias_in.reshape(1, HID),
        jnp.transpose(conv_out, (2, 3, 0, 1)).reshape(9 * FIELDS, HID),
        bias_out.reshape(1, FIELDS),
        index.reshape(1, SLOTS),
    )


def forecast_kernel(
    x_ref,
    base_ref,
    top_ref,
    bottom_ref,
    first_top_ref,
    first_bottom_ref,
    low_ref,
    middle_ref,
    high_ref,
    bias_ref,
    picks_ref,
    plane_ref,
    earlier_ref,
    fields_ref,
    observed_ref,
    held_ref,
):
    step = pl.program_id(0)
    ones = jnp.ones((16, RING), jnp.bfloat16)
    part = PLANES // 2

    def changes(member):
        stack = jnp.concatenate(
            [
                top_ref[member].reshape(2 * FIELDS, LON),
                x_ref[member].reshape(PLANES, LON),
                bottom_ref[member].reshape(2 * FIELDS, LON),
            ],
            axis=0,
        )
        ring = jnp.concatenate([stack, stack[:, :64], stack[:, LON - 32 :]], axis=1)
        left = pltpu.roll(ring, 1, 1)
        right = pltpu.roll(ring, RING - 1, 1)

        def hidden_rows(at, weights_ref):
            to = at + 5 * FIELDS
            taps = jnp.concatenate([left[at:to], ring[at:to], right[at:to], ones], axis=0)
            half = jnp.dot(weights_ref[...], taps, preferred_element_type=jnp.float32)
            return (half * jnp.tanh(half) + half).astype(jnp.bfloat16)

        hidden = jnp.concatenate(
            [hidden_rows(0, first_top_ref), hidden_rows(3 * FIELDS, first_bottom_ref)], axis=0
        )

        def outer(weights_ref, pair):
            rows = hidden[2 * HID * pair : 2 * HID * (pair + 1)]
            return jnp.dot(weights_ref[...], rows, preferred_element_type=jnp.float32)

        both = outer(middle_ref, 1)
        for taps in (both[: 3 * part] + outer(low_ref, 0), both[3 * part :] + outer(high_ref, 2)):
            yield (
                pltpu.roll(taps[:part], 1, 1)
                + taps[part : 2 * part]
                + pltpu.roll(taps[2 * part :], RING - 1, 1)
            )

    sub = lax.broadcasted_iota(jnp.int32, (8, RING), 0)
    pairs = []
    for pair in range(STEP // 2):
        sources = [*changes(2 * pair), *changes(2 * pair + 1)]
        blocks = []
        for field in range(FIELDS):
            at, by = field // 4 * 8, field % 4 * 2
            moved = [
                pltpu.roll(source[at : at + 8], (2 * k - by) % 8, 0) if (2 * k - by) % 8 else source[at : at + 8]
                for k, source in enumerate(sources)
            ]
            first = jnp.where(sub < 2, moved[0], moved[1])
            last = jnp.where(sub < 6, moved[2], moved[3])
            blocks.append(jnp.where(sub < 4, first, last))
        pairs.append(blocks)
    for field in range(FIELDS):
        low, high = field * 16, field * 16 + 16
        base = base_ref[0, low:high, :].astype(jnp.float32) + bias_ref[low:high, :]
        base = jnp.concatenate([base, base[:, : RING - LON]], axis=1)
        change = jnp.concatenate([blocks[field] for blocks in pairs], axis=0)
        own = (base + change).astype(jnp.bfloat16)
        fields_ref[field // 2, field % 2] = own[:, :LON]
        held_ref[pl.ds(pl.multiple_of(step * 16 * FIELDS + low, 16), 16), :] = own

    @pl.when(step == pl.num_programs(0) - 1)
    def _():
        rows = held_ref.shape[0]
        picked = jnp.dot(held_ref[...], picks_ref[...], preferred_element_type=jnp.float32)
        row = lax.broadcasted_iota(jnp.int32, (rows, SLOTS), 0)
        here = row % 256 // 16 * ROWS + row % ROWS == plane_ref[...]
        found = jnp.where(here, picked, 0.0).astype(jnp.bfloat16)
        count = rows // PLANES
        column = lax.broadcasted_iota(jnp.int32, (count, rows), 1)
        member = column // 256 * STEP + column % 16 // ROWS
        mine = member == lax.broadcasted_iota(jnp.int32, (count, rows), 0)
        seen = jnp.dot(
            mine.astype(jnp.bfloat16), found, preferred_element_type=jnp.float32
        )
        if earlier_ref is not None:
            seen = jnp.concatenate([earlier_ref[...], seen], axis=0)
        observed_ref[...] = seen


def cost(microseconds):
    return pl.CostEstimate(
        flops=int(microseconds * 1e9), transcendentals=0, bytes_accessed=int(microseconds * 1e6)
    )


def forecast(start, own, base, top, bottom, shared, earlier):
    count = top.shape[0]
    steps = count // STEP
    first = start // STEP
    whole = lambda array: pl.BlockSpec(array.shape, lambda m: (0,) * array.ndim)
    kernel = forecast_kernel
    if earlier is None:
        kernel = lambda *refs: forecast_kernel(*refs[:-3], None, *refs[-3:])
        seen = count
    else:
        shared = [*shared, earlier]
        seen = count + earlier.shape[0]
    return pl.pallas_call(
        kernel,
        grid=(steps,),
        in_specs=[
            pl.BlockSpec((STEP, ROWS, FIELDS, LON), lambda m: (first + m, 0, 0, 0)),
            pl.BlockSpec((1, 16 * FIELDS, LON), lambda m: (first + m, 0, 0)),
            pl.BlockSpec((STEP, 2, FIELDS, LON), lambda m: (m, 0, 0, 0)),
            pl.BlockSpec((STEP, 2, FIELDS, LON), lambda m: (m, 0, 0, 0)),
        ]
        + [whole(array) for array in shared],
        out_specs=[
            pl.BlockSpec((N_ENS, 2, 16, LON), lambda m: (0, 0, m, 0)),
            pl.BlockSpec((seen, SLOTS), lambda m: (0, 0)),
        ],
        out_shape=[
            jax.ShapeDtypeStruct((N_ENS, 2, count * ROWS, LON), jnp.bfloat16),
            jax.ShapeDtypeStruct((seen, SLOTS), jnp.float32),
        ],
        scratch_shapes=[pltpu.VMEM((count * PLANES, RING), jnp.bfloat16)],
        cost_estimate=cost(2 * count),
        compiler_params=pltpu.CompilerParams(vmem_limit_bytes=VMEM_LIMIT),
    )(own, base, top, bottom, *shared)


def products_kernel(place_ref, count_ref, value_ref, sigma_ref, *refs):
    pieces, out_ref, held_ref = refs[:N_ENS], refs[N_ENS], refs[N_ENS + 1]
    for step, piece in enumerate(pieces):
        at = pl.multiple_of((place_ref[0] ^ step) * GROUP, GROUP)
        held_ref[pl.ds(at, GROUP), :] = piece[...]
    observed = held_ref[...]
    mean = jnp.sum(observed, axis=0, keepdims=True) / MEMBERS
    slot = lax.broadcasted_iota(jnp.int32, (1, SLOTS), 1)
    live = (slot < count_ref[0]).astype(jnp.float32)
    sigma = sigma_ref[...]
    anomalies = (observed - mean) * (live / (sigma * math.sqrt(MEMBERS - 1)))
    innov = live * (value_ref[...] - mean) / sigma
    left = jnp.concatenate([anomalies, jnp.broadcast_to(innov, (8, SLOTS))], axis=0)
    out_ref[...] = lax.dot_general(
        left,
        anomalies,
        (((1,), (1,)), ((), ())),
        precision=lax.Precision.HIGHEST,
        preferred_element_type=jnp.float32,
    )


def products(pieces, places, count, value, sigma):
    vmem = pl.BlockSpec(memory_space=pltpu.VMEM)
    smem = pl.BlockSpec(memory_space=pltpu.SMEM)
    return pl.pallas_call(
        products_kernel,
        in_specs=[smem, smem] + [vmem] * (2 + N_ENS),
        out_specs=vmem,
        out_shape=jax.ShapeDtypeStruct((MEMBERS + 8, MEMBERS), jnp.float32),
        cost_estimate=cost(1),
        scratch_shapes=[pltpu.VMEM((MEMBERS, SLOTS), jnp.float32)],
    )(places, count, value.reshape(1, SLOTS), sigma.reshape(1, SLOTS), *pieces)


def transform_kernel(a_ref, b_ref, c_ref, d_ref, factor_ref, weights_ref, transform_ref):
    n = MEMBERS
    total = (a_ref[...] + b_ref[...]) + (c_ref[...] + d_ref[...])
    row = lax.broadcasted_iota(jnp.int32, (n, n), 0)
    column = lax.broadcasted_iota(jnp.int32, (n, n), 1)
    eye = (row == column).astype(jnp.float32)
    gram = total[0:n] + eye
    blocks = [[gram[b : b + 8], eye[b : b + 8]] for b in range(0, n, 8)]
    within = lax.broadcasted_iota(jnp.int32, (8, n), 0)
    wide = lambda value: jnp.broadcast_to(value, (8, n))
    for b in range(n // 8):
        upper, inverse = blocks[b]
        columns = [wide(upper[:, 8 * b + k : 8 * b + k + 1]) for k in range(8)]
        scales, steps, rows = [], [], []
        for k in range(8):
            scale = lax.rsqrt(wide(columns[k][k : k + 1]))
            share = columns[k] * scale
            step = {}
            for later in range(k + 1, 8):
                step[later] = wide(share[later : later + 1])
                columns[later] = columns[later] - share * step[later]
            upper_row = wide(upper[k : k + 1]) * scale
            inverse_row = wide(inverse[k : k + 1]) * scale
            share = jnp.where(within > k, share, 0.0)
            upper = jnp.where(within == k, upper_row, upper - share * upper_row)
            inverse = jnp.where(within == k, inverse_row, inverse - share * inverse_row)
            scales.append(scale)
            steps.append(step)
            rows.append((upper_row, inverse_row))
        for t in range(b + 1, n // 8):
            later_upper, later_inverse = blocks[t]
            columns = [wide(later_upper[:, 8 * b + k : 8 * b + k + 1]) for k in range(8)]
            for k in range(8):
                share = columns[k] * scales[k]
                for later in range(k + 1, 8):
                    columns[later] = columns[later] - share * steps[k][later]
                later_upper = later_upper - share * rows[k][0]
                later_inverse = later_inverse - share * rows[k][1]
            blocks[t] = [later_upper, later_inverse]
        blocks[b] = [upper, inverse]
    upper = jnp.concatenate([pair[0] for pair in blocks], axis=0)
    inverse = jnp.concatenate([pair[1] for pair in blocks], axis=0)
    factor_ref[...] = jnp.where(row <= column, upper, 0.0).T
    proj = total[n : n + 1]
    middle = jnp.sum(inverse * proj, axis=1, keepdims=True)
    weights = jnp.sum(inverse * middle, axis=0, keepdims=True) / math.sqrt(n - 1)
    weights_ref[...] = weights
    coeff = inverse + weights
    transform = coeff - jnp.mean(coeff, axis=1, keepdims=True) + 1.0 / n
    transform_ref[...] = transform.astype(jnp.bfloat16)


def transform_of(parts):
    vmem = pl.BlockSpec(memory_space=pltpu.VMEM)
    return pl.pallas_call(
        transform_kernel,
        in_specs=[vmem] * 4,
        out_specs=[vmem, vmem, vmem],
        out_shape=[
            jax.ShapeDtypeStruct((MEMBERS, MEMBERS), jnp.float32),
            jax.ShapeDtypeStruct((1, MEMBERS), jnp.float32),
            jax.ShapeDtypeStruct((MEMBERS, MEMBERS), jnp.bfloat16),
        ],
        cost_estimate=cost(1),
    )(*parts)


def update_kernel(transform_ref, early_ref, late_ref, out_ref, spread_ref):
    rows = MEMBERS * ROWS
    half = rows // 2

    @pl.when((pl.program_id(0) == 0) & (pl.program_id(1) == 0))
    def _():
        shape = (rows, MEMBERS)
        row = lax.broadcasted_iota(jnp.int32, shape, 0)
        column = lax.broadcasted_iota(jnp.int32, shape, 1)
        held = row % half // 32 * GROUP + row // half * 8 + row % 32 // ROWS
        wanted = row // 64 * GROUP + row % GROUP
        repeat = (wanted == column).astype(jnp.bfloat16)
        placed = (held == column).astype(jnp.bfloat16)
        tall = jnp.dot(repeat, transform_ref[...], preferred_element_type=jnp.float32)
        wide = lax.dot_general(
            tall.astype(jnp.bfloat16),
            placed,
            (((1,), (1,)), ((), ())),
            preferred_element_type=jnp.float32,
        )
        own = lax.broadcasted_iota(jnp.int32, (rows, rows), 0) // GROUP % ROWS
        same = own == lax.broadcasted_iota(jnp.int32, (rows, rows), 1) % ROWS
        spread_ref[...] = jnp.where(same, wide, 0.0).astype(jnp.bfloat16)

    width = early_ref.shape[-1]
    fields = jnp.concatenate(
        [early_ref[:, 0].reshape(half, width), late_ref[:, 0].reshape(half, width)], axis=0
    )
    mixed = jnp.dot(spread_ref[...], fields, preferred_element_type=jnp.float32)
    out_ref[:, 0] = mixed.astype(jnp.bfloat16).reshape(N_ENS, GROUP * ROWS, width)


def update(transform, early, late):
    rows = MEMBERS * ROWS
    half = pl.BlockSpec((N_ENS, 1, 8 * ROWS, RING // 2), lambda c, x: (0, c, 0, x))
    return pl.pallas_call(
        update_kernel,
        grid=(2, 2),
        in_specs=[pl.BlockSpec((MEMBERS, MEMBERS), lambda c, x: (0, 0)), half, half],
        out_specs=pl.BlockSpec(
            (N_ENS, 1, GROUP * ROWS, RING // 2), lambda c, x: (0, c, 0, x)
        ),
        out_shape=jax.ShapeDtypeStruct((N_ENS, 2, GROUP * ROWS, LON), jnp.bfloat16),
        scratch_shapes=[pltpu.VMEM((rows, rows), jnp.bfloat16)],
        cost_estimate=cost(4),
        compiler_params=pltpu.CompilerParams(vmem_limit_bytes=VMEM_LIMIT),
    )(transform, early, late)


def on_device(
    ensemble_weather,
    conv_in,
    bias_in,
    conv_out,
    bias_out,
    observed_entry_index,
    obs_count,
    obs_value,
    obs_sigma,
):
    tiles = lax.axis_size("map")
    tile = lax.axis_index("map")
    own_place = lax.axis_index("ens")
    down = [(i, i + 1) for i in range(tiles - 1)]
    up = [(i + 1, i) for i in range(tiles - 1)]

    def swap(value, axis, step):
        pairs = [(i, i ^ step) for i in range(lax.axis_size(axis))]
        return lax.ppermute(value, axis, pairs)

    share = GROUP // CHUNKS
    exchange = lambda value: lax.all_to_all(
        value, "ens", split_axis=0, concat_axis=0, tiled=True
    )
    own = jnp.transpose(ensemble_weather, (0, 2, 1, 3))

    def edges(chunk):
        part = own[chunk * share : (chunk + 1) * share]
        return part[:, ROWS - 2 :], part[:, :2]

    def halo(rows):
        return lax.ppermute(rows[0], "map", down), lax.ppermute(rows[1], "map", up)

    halos = [halo(edges(0))]
    shared = prepare(
        tile, tiles, conv_in, bias_in, conv_out, bias_out, observed_entry_index
    )
    base = jnp.transpose(
        ensemble_weather.reshape(GROUP // STEP, STEP, FIELDS, ROWS, LON), (0, 2, 1, 3, 4)
    ).reshape(GROUP // STEP, STEP * PLANES, LON)
    next_edges, shared, base = lax.optimization_barrier((edges(1), shared, base))
    halos.append(halo(next_edges))
    fields, observed = [], None
    for chunk, (top, bottom) in enumerate(halos):
        moved, observed = forecast(chunk * share, own, base, top, bottom, shared, observed)
        fields.append(moved)
    early = exchange(fields[0])
    pieces = [observed] + [swap(observed, "ens", step) for step in range(1, N_ENS)]
    places = own_place.astype(jnp.int32).reshape(1)
    pieces, late, early = lax.optimization_barrier((pieces, fields[1], early))
    late = exchange(late)
    part = products(pieces, places, obs_count, obs_value, obs_sigma)
    near = [part] + [swap(part, "map", step) for step in (1, 2, 3)]
    row = (near[0] + near[1]) + (near[2] + near[3])
    factor, mean_weights, transform = transform_of(
        [row] + [swap(row, "map", step) for step in (4, 8, 12)]
    )
    back = exchange(update(transform, early, late))
    back = back.reshape(FIELDS, ROWS, GROUP, LON)
    analysis = jnp.transpose(back, (2, 0, 1, 3))
    return (analysis, factor, mean_weights.reshape(MEMBERS))


def solution(mesh):
    placed = (
        P("ens", None, "map", None),
        P(),
        P(),
        P(),
        P(),
        P("map"),
        P("map"),
        P("map"),
        P("map"),
    )
    return jax.shard_map(
        on_device,
        mesh=mesh,
        in_specs=placed,
        out_specs=(P("ens", None, "map", None), P(), P()),
        check_vma=False,
    )
```

```python
import functools
import math

import jax
import jax.numpy as jnp
from jax import lax
from jax.experimental import pallas as pl
from jax.experimental.pallas import tpu as pltpu
from jax.sharding import PartitionSpec as P

FIELDS = 16
HID = 128
ROWS = 4
LON = 1440
RING = 1536
SLOTS = 256
GROUP = 16
PLANES = ROWS * FIELDS
CHUNKS = 2
STEP = 4
N_ENS = 8
MEMBERS = 128
VMEM_LIMIT = 56 * 1024 * 1024


def prepare_kernel(
    tile_ref,
    first_ref,
    bias_in_ref,
    second_ref,
    bias_out_ref,
    index_ref,
    top_ref,
    bottom_ref,
    low_ref,
    middle_ref,
    high_ref,
    bias_ref,
    picks_ref,
    plane_ref,
    *,
    tiles,
):
    tap = lambda ref, row, column: ref[(3 * row + column) * 16 : (3 * row + column + 1) * 16]
    half = bias_in_ref[...] * 0.5
    high = half.astype(jnp.bfloat16).astype(jnp.float32)
    middle = (half - high).astype(jnp.bfloat16).astype(jnp.float32)
    low = half - high - middle
    zeros = jnp.zeros((16, HID), jnp.float32)
    bias = jnp.concatenate([high, middle, low, zeros[:13]], axis=0)
    parts = []
    for r in range(3):
        pieces = []
        for column in range(3):
            for row in range(5):
                known = 0 <= row - r <= 2
                piece = tap(first_ref, row - r, column).astype(jnp.float32) if known else zeros
                pieces.append(piece * 0.5)
        parts.append(jnp.concatenate(pieces + [bias], axis=0).T)
    tile = tile_ref[0]
    inner_top = jnp.where(tile > 0, 1.0, 0.0)
    inner_bottom = jnp.where(tile < tiles - 1, 1.0, 0.0)
    top = jnp.concatenate([parts[0] * inner_top, parts[1], parts[2]], axis=0)
    bottom = jnp.concatenate([parts[0], parts[1], parts[2] * inner_bottom], axis=0)
    top_ref[...] = top.astype(jnp.bfloat16)
    bottom_ref[...] = bottom.astype(jnp.bfloat16)

    rows = 6 * FIELDS
    to = lax.broadcasted_iota(jnp.int32, (rows, rows), 0)
    source = to // 32 * 32 + to % 2 * 16 + to % 32 // 2
    turn = (source == lax.broadcasted_iota(jnp.int32, (rows, rows), 1)).astype(jnp.bfloat16)

    def placed(taps):
        blank = jnp.zeros((16, HID), jnp.bfloat16)
        lines = []
        for column in range(3):
            for line in taps:
                cells = [blank if d is None else tap(second_ref, d, column) for d in line]
                lines.append(jnp.concatenate(cells, axis=1))
        whole = jnp.concatenate(lines, axis=0)
        return jnp.dot(turn, whole, preferred_element_type=jnp.float32).astype(jnp.bfloat16)

    upper = placed(((0, 1), (None, 0)))
    lower = placed(((2, None), (1, 2)))
    low_ref[...] = upper
    middle_ref[...] = jnp.concatenate([lower, upper], axis=0)
    high_ref[...] = lower

    group = 16 * FIELDS
    field = lax.broadcasted_iota(jnp.int32, (group, FIELDS), 0) // 16
    mine = field == lax.broadcasted_iota(jnp.int32, (group, FIELDS), 1)
    bias_ref[...] = jnp.sum(jnp.where(mine, bias_out_ref[...], 0.0), axis=1, keepdims=True)

    entry = index_ref[...]
    bound = (lax.broadcasted_iota(jnp.int32, (PLANES, SLOTS), 0) + 1) * LON
    plane = jnp.sum(jnp.where(entry >= bound, 1, 0), axis=0, keepdims=True)
    plane_ref[...] = plane
    column = entry - plane * LON
    for at in range(0, RING, 256):
        place = lax.broadcasted_iota(jnp.int32, (256, SLOTS), 0) + at
        picks_ref[at : at + 256, :] = jnp.where(place == column, 1.0, 0.0).astype(jnp.bfloat16)


def prepare(tile, tiles, conv_in, bias_in, conv_out, bias_out, index):
    vmem = pl.BlockSpec(memory_space=pltpu.VMEM)
    shape = jax.ShapeDtypeStruct
    return pl.pallas_call(
        functools.partial(prepare_kernel, tiles=tiles),
        in_specs=[pl.BlockSpec(memory_space=pltpu.SMEM)] + [vmem] * 5,
        out_specs=[vmem] * 8,
        out_shape=[
            shape((3 * HID, 256), jnp.bfloat16),
            shape((3 * HID, 256), jnp.bfloat16),
            shape((6 * FIELDS, 2 * HID), jnp.bfloat16),
            shape((12 * FIELDS, 2 * HID), jnp.bfloat16),
            shape((6 * FIELDS, 2 * HID), jnp.bfloat16),
            shape((16 * FIELDS, 1), jnp.float32),
            shape((RING, SLOTS), jnp.bfloat16),
            shape((1, SLOTS), jnp.int32),
        ],
        cost_estimate=cost(3),
    )(
        tile.astype(jnp.int32).reshape(1),
        jnp.transpose(conv_in, (2, 3, 1, 0)).reshape(9 * FIELDS, HID),
        bias_in.reshape(1, HID),
        jnp.transpose(conv_out, (2, 3, 0, 1)).reshape(9 * FIELDS, HID),
        bias_out.reshape(1, FIELDS),
        index.reshape(1, SLOTS),
    )


def forecast_kernel(
    x_ref,
    base_ref,
    top_ref,
    bottom_ref,
    first_top_ref,
    first_bottom_ref,
    low_ref,
    middle_ref,
    high_ref,
    bias_ref,
    picks_ref,
    plane_ref,
    earlier_ref,
    fields_ref,
    observed_ref,
    held_ref,
):
    step = pl.program_id(0)
    ones = jnp.ones((16, RING), jnp.bfloat16)
    part = PLANES // 2

    def changes(member):
        stack = jnp.concatenate(
            [
                top_ref[member].reshape(2 * FIELDS, LON),
                x_ref[member].reshape(PLANES, LON),
                bottom_ref[member].reshape(2 * FIELDS, LON),
            ],
            axis=0,
        )
        ring = jnp.concatenate([stack, stack[:, :64], stack[:, LON - 32 :]], axis=1)
        left = pltpu.roll(ring, 1, 1)
        right = pltpu.roll(ring, RING - 1, 1)

        def hidden_rows(at, weights_ref):
            to = at + 5 * FIELDS
            taps = jnp.concatenate([left[at:to], ring[at:to], right[at:to], ones], axis=0)
            half = jnp.dot(weights_ref[...], taps, preferred_element_type=jnp.float32)
            return (half * jnp.tanh(half) + half).astype(jnp.bfloat16)

        hidden = jnp.concatenate(
            [hidden_rows(0, first_top_ref), hidden_rows(3 * FIELDS, first_bottom_ref)], axis=0
        )

        def outer(weights_ref, pair):
            rows = hidden[2 * HID * pair : 2 * HID * (pair + 1)]
            return jnp.dot(weights_ref[...], rows, preferred_element_type=jnp.float32)

        both = outer(middle_ref, 1)
        for taps in (both[: 3 * part] + outer(low_ref, 0), both[3 * part :] + outer(high_ref, 2)):
            yield (
                pltpu.roll(taps[:part], 1, 1)
                + taps[part : 2 * part]
                + pltpu.roll(taps[2 * part :], RING - 1, 1)
            )

    sub = lax.broadcasted_iota(jnp.int32, (8, RING), 0)
    pairs = []
    for pair in range(STEP // 2):
        sources = [*changes(2 * pair), *changes(2 * pair + 1)]
        blocks = []
        for field in range(FIELDS):
            at, by = field // 4 * 8, field % 4 * 2
            moved = [
                pltpu.roll(source[at : at + 8], (2 * k - by) % 8, 0) if (2 * k - by) % 8 else source[at : at + 8]
                for k, source in enumerate(sources)
            ]
            first = jnp.where(sub < 2, moved[0], moved[1])
            last = jnp.where(sub < 6, moved[2], moved[3])
            blocks.append(jnp.where(sub < 4, first, last))
        pairs.append(blocks)
    for field in range(FIELDS):
        low, high = field * 16, field * 16 + 16
        base = base_ref[0, low:high, :].astype(jnp.float32) + bias_ref[low:high, :]
        base = jnp.concatenate([base, base[:, : RING - LON]], axis=1)
        change = jnp.concatenate([blocks[field] for blocks in pairs], axis=0)
        own = (base + change).astype(jnp.bfloat16)
        fields_ref[field // 2, field % 2] = own[:, :LON]
        held_ref[pl.ds(pl.multiple_of(step * 16 * FIELDS + low, 16), 16), :] = own

    @pl.when(step == pl.num_programs(0) - 1)
    def _():
        rows = held_ref.shape[0]
        picked = jnp.dot(held_ref[...], picks_ref[...], preferred_element_type=jnp.float32)
        row = lax.broadcasted_iota(jnp.int32, (rows, SLOTS), 0)
        here = row % 256 // 16 * ROWS + row % ROWS == plane_ref[...]
        found = jnp.where(here, picked, 0.0).astype(jnp.bfloat16)
        count = rows // PLANES
        column = lax.broadcasted_iota(jnp.int32, (count, rows), 1)
        member = column // 256 * STEP + column % 16 // ROWS
        mine = member == lax.broadcasted_iota(jnp.int32, (count, rows), 0)
        seen = jnp.dot(
            mine.astype(jnp.bfloat16), found, preferred_element_type=jnp.float32
        )
        if earlier_ref is not None:
            seen = jnp.concatenate([earlier_ref[...], seen], axis=0)
        observed_ref[...] = seen


def cost(microseconds):
    return pl.CostEstimate(
        flops=int(microseconds * 1e9), transcendentals=0, bytes_accessed=int(microseconds * 1e6)
    )


def forecast(start, own, base, top, bottom, shared, earlier):
    count = top.shape[0]
    steps = count // STEP
    first = start // STEP
    whole = lambda array: pl.BlockSpec(array.shape, lambda m: (0,) * array.ndim)
    kernel = forecast_kernel
    if earlier is None:
        kernel = lambda *refs: forecast_kernel(*refs[:-3], None, *refs[-3:])
        seen = count
    else:
        shared = [*shared, earlier]
        seen = count + earlier.shape[0]
    return pl.pallas_call(
        kernel,
        grid=(steps,),
        in_specs=[
            pl.BlockSpec((STEP, ROWS, FIELDS, LON), lambda m: (first + m, 0, 0, 0)),
            pl.BlockSpec((1, 16 * FIELDS, LON), lambda m: (first + m, 0, 0)),
            pl.BlockSpec((STEP, 2, FIELDS, LON), lambda m: (m, 0, 0, 0)),
            pl.BlockSpec((STEP, 2, FIELDS, LON), lambda m: (m, 0, 0, 0)),
        ]
        + [whole(array) for array in shared],
        out_specs=[
            pl.BlockSpec((N_ENS, 2, 16, LON), lambda m: (0, 0, m, 0)),
            pl.BlockSpec((seen, SLOTS), lambda m: (0, 0)),
        ],
        out_shape=[
            jax.ShapeDtypeStruct((N_ENS, 2, count * ROWS, LON), jnp.bfloat16),
            jax.ShapeDtypeStruct((seen, SLOTS), jnp.float32),
        ],
        scratch_shapes=[pltpu.VMEM((count * PLANES, RING), jnp.bfloat16)],
        cost_estimate=cost(2 * count),
        compiler_params=pltpu.CompilerParams(vmem_limit_bytes=VMEM_LIMIT),
    )(own, base, top, bottom, *shared)


def products_kernel(place_ref, count_ref, value_ref, sigma_ref, *refs):
    pieces, out_ref, held_ref = refs[: N_ENS // 2], refs[N_ENS // 2], refs[N_ENS // 2 + 1]
    for step in range(N_ENS):
        at = pl.multiple_of((place_ref[0] ^ step) * GROUP, GROUP)
        low = step % 2 * GROUP
        held_ref[pl.ds(at, GROUP), :] = pieces[step // 2][low : low + GROUP, :]
    observed = held_ref[...]
    mean = jnp.sum(observed, axis=0, keepdims=True) / MEMBERS
    slot = lax.broadcasted_iota(jnp.int32, (1, SLOTS), 1)
    live = (slot < count_ref[0]).astype(jnp.float32)
    sigma = sigma_ref[...]
    anomalies = (observed - mean) * (live / (sigma * math.sqrt(MEMBERS - 1)))
    innov = live * (value_ref[...] - mean) / sigma
    left = jnp.concatenate([anomalies, jnp.broadcast_to(innov, (8, SLOTS))], axis=0)
    out_ref[...] = lax.dot_general(
        left,
        anomalies,
        (((1,), (1,)), ((), ())),
        precision=lax.Precision.HIGHEST,
        preferred_element_type=jnp.float32,
    )


def products(pieces, places, count, value, sigma):
    vmem = pl.BlockSpec(memory_space=pltpu.VMEM)
    smem = pl.BlockSpec(memory_space=pltpu.SMEM)
    return pl.pallas_call(
        products_kernel,
        in_specs=[smem, smem] + [vmem] * (2 + N_ENS // 2),
        out_specs=vmem,
        out_shape=jax.ShapeDtypeStruct((MEMBERS + 8, MEMBERS), jnp.float32),
        cost_estimate=cost(1),
        scratch_shapes=[pltpu.VMEM((MEMBERS, SLOTS), jnp.float32)],
    )(places, count, value.reshape(1, SLOTS), sigma.reshape(1, SLOTS), *pieces)


def transform_kernel(a_ref, b_ref, c_ref, d_ref, factor_ref, weights_ref, transform_ref):
    n = MEMBERS
    total = (a_ref[...] + b_ref[...]) + (c_ref[...] + d_ref[...])
    row = lax.broadcasted_iota(jnp.int32, (n, n), 0)
    column = lax.broadcasted_iota(jnp.int32, (n, n), 1)
    eye = (row == column).astype(jnp.float32)
    gram = total[0:n] + eye
    blocks = [[gram[b : b + 8], eye[b : b + 8]] for b in range(0, n, 8)]
    within = lax.broadcasted_iota(jnp.int32, (8, n), 0)
    wide = lambda value: jnp.broadcast_to(value, (8, n))
    for b in range(n // 8):
        upper, inverse = blocks[b]
        columns = [wide(upper[:, 8 * b + k : 8 * b + k + 1]) for k in range(8)]
        scales, steps, rows = [], [], []
        for k in range(8):
            scale = lax.rsqrt(wide(columns[k][k : k + 1]))
            share = columns[k] * scale
            step = {}
            for later in range(k + 1, 8):
                step[later] = wide(share[later : later + 1])
                columns[later] = columns[later] - share * step[later]
            upper_row = wide(upper[k : k + 1]) * scale
            inverse_row = wide(inverse[k : k + 1]) * scale
            share = jnp.where(within > k, share, 0.0)
            upper = jnp.where(within == k, upper_row, upper - share * upper_row)
            inverse = jnp.where(within == k, inverse_row, inverse - share * inverse_row)
            scales.append(scale)
            steps.append(step)
            rows.append((upper_row, inverse_row))
        for t in range(b + 1, n // 8):
            later_upper, later_inverse = blocks[t]
            columns = [wide(later_upper[:, 8 * b + k : 8 * b + k + 1]) for k in range(8)]
            for k in range(8):
                share = columns[k] * scales[k]
                for later in range(k + 1, 8):
                    columns[later] = columns[later] - share * steps[k][later]
                later_upper = later_upper - share * rows[k][0]
                later_inverse = later_inverse - share * rows[k][1]
            blocks[t] = [later_upper, later_inverse]
        blocks[b] = [upper, inverse]
    upper = jnp.concatenate([pair[0] for pair in blocks], axis=0)
    inverse = jnp.concatenate([pair[1] for pair in blocks], axis=0)
    factor_ref[...] = jnp.where(row <= column, upper, 0.0).T
    proj = total[n : n + 1]
    middle = jnp.sum(inverse * proj, axis=1, keepdims=True)
    weights = jnp.sum(inverse * middle, axis=0, keepdims=True) / math.sqrt(n - 1)
    weights_ref[...] = weights
    coeff = inverse + weights
    transform = coeff - jnp.mean(coeff, axis=1, keepdims=True) + 1.0 / n
    transform_ref[...] = transform.astype(jnp.bfloat16)


def transform_of(parts):
    vmem = pl.BlockSpec(memory_space=pltpu.VMEM)
    return pl.pallas_call(
        transform_kernel,
        in_specs=[vmem] * 4,
        out_specs=[vmem, vmem, vmem],
        out_shape=[
            jax.ShapeDtypeStruct((MEMBERS, MEMBERS), jnp.float32),
            jax.ShapeDtypeStruct((1, MEMBERS), jnp.float32),
            jax.ShapeDtypeStruct((MEMBERS, MEMBERS), jnp.bfloat16),
        ],
        cost_estimate=cost(1),
        compiler_params=pltpu.CompilerParams(vmem_limit_bytes=60 * 1024 * 1024),
    )(*parts)


def update_kernel(transform_ref, early_ref, late_ref, out_ref, spread_ref):
    rows = MEMBERS * ROWS
    half = rows // 2

    @pl.when((pl.program_id(0) == 0) & (pl.program_id(1) == 0))
    def _():
        shape = (rows, MEMBERS)
        row = lax.broadcasted_iota(jnp.int32, shape, 0)
        column = lax.broadcasted_iota(jnp.int32, shape, 1)
        held = row % half // 32 * GROUP + row // half * 8 + row % 32 // ROWS
        wanted = row // 64 * GROUP + row % GROUP
        repeat = (wanted == column).astype(jnp.bfloat16)
        placed = (held == column).astype(jnp.bfloat16)
        tall = jnp.dot(repeat, transform_ref[...], preferred_element_type=jnp.float32)
        wide = lax.dot_general(
            tall.astype(jnp.bfloat16),
            placed,
            (((1,), (1,)), ((), ())),
            preferred_element_type=jnp.float32,
        )
        own = lax.broadcasted_iota(jnp.int32, (rows, rows), 0) // GROUP % ROWS
        same = own == lax.broadcasted_iota(jnp.int32, (rows, rows), 1) % ROWS
        spread_ref[...] = jnp.where(same, wide, 0.0).astype(jnp.bfloat16)

    width = early_ref.shape[-1]
    fields = jnp.concatenate(
        [early_ref[:, 0].reshape(half, width), late_ref[:, 0].reshape(half, width)], axis=0
    )
    mixed = jnp.dot(spread_ref[...], fields, preferred_element_type=jnp.float32)
    out_ref[:, 0] = mixed.astype(jnp.bfloat16).reshape(N_ENS, GROUP * ROWS, width)


def update(transform, early, late):
    rows = MEMBERS * ROWS
    half = pl.BlockSpec((N_ENS, 1, 8 * ROWS, RING // 2), lambda c, x: (0, c, 0, x))
    return pl.pallas_call(
        update_kernel,
        grid=(2, 2),
        in_specs=[pl.BlockSpec((MEMBERS, MEMBERS), lambda c, x: (0, 0)), half, half],
        out_specs=pl.BlockSpec(
            (N_ENS, 1, GROUP * ROWS, RING // 2), lambda c, x: (0, c, 0, x)
        ),
        out_shape=jax.ShapeDtypeStruct((N_ENS, 2, GROUP * ROWS, LON), jnp.bfloat16),
        scratch_shapes=[pltpu.VMEM((rows, rows), jnp.bfloat16)],
        cost_estimate=cost(4),
        compiler_params=pltpu.CompilerParams(vmem_limit_bytes=VMEM_LIMIT),
    )(transform, early, late)


def on_device(
    ensemble_weather,
    conv_in,
    bias_in,
    conv_out,
    bias_out,
    observed_entry_index,
    obs_count,
    obs_value,
    obs_sigma,
):
    tiles = lax.axis_size("map")
    tile = lax.axis_index("map")
    own_place = lax.axis_index("ens")
    down = [(i, i + 1) for i in range(tiles - 1)]
    up = [(i + 1, i) for i in range(tiles - 1)]

    def swap(value, axis, step):
        pairs = [(i, i ^ step) for i in range(lax.axis_size(axis))]
        return lax.ppermute(value, axis, pairs)

    share = GROUP // CHUNKS
    exchange = lambda value: lax.all_to_all(
        value, "ens", split_axis=0, concat_axis=0, tiled=True
    )
    own = jnp.transpose(ensemble_weather, (0, 2, 1, 3))

    def edges(chunk):
        part = own[chunk * share : (chunk + 1) * share]
        return part[:, ROWS - 2 :], part[:, :2]

    def halo(rows):
        return lax.ppermute(rows[0], "map", down), lax.ppermute(rows[1], "map", up)

    halos = [halo(edges(0))]
    shared = prepare(
        tile, tiles, conv_in, bias_in, conv_out, bias_out, observed_entry_index
    )
    base = jnp.transpose(
        ensemble_weather.reshape(GROUP // STEP, STEP, FIELDS, ROWS, LON), (0, 2, 1, 3, 4)
    ).reshape(GROUP // STEP, STEP * PLANES, LON)
    next_edges, shared, base = lax.optimization_barrier((edges(1), shared, base))
    halos.append(halo(next_edges))
    fields, observed = [], None
    for chunk, (top, bottom) in enumerate(halos):
        moved, observed = forecast(chunk * share, own, base, top, bottom, shared, observed)
        fields.append(moved)
    early = exchange(fields[0])
    observed = jnp.concatenate([observed, swap(observed, "ens", 1)], axis=0)
    pieces = [observed] + [swap(observed, "ens", step) for step in range(2, N_ENS, 2)]
    places = own_place.astype(jnp.int32).reshape(1)
    pieces, late, early = lax.optimization_barrier((pieces, fields[1], early))
    late = exchange(late)
    part = products(pieces, places, obs_count, obs_value, obs_sigma)
    near = [part] + [swap(part, "map", step) for step in (1, 2, 3)]
    row = (near[0] + near[1]) + (near[2] + near[3])
    factor, mean_weights, transform = transform_of(
        [row] + [swap(row, "map", step) for step in (4, 8, 12)]
    )
    back = exchange(update(transform, early, late))
    back = back.reshape(FIELDS, ROWS, GROUP, LON)
    analysis = jnp.transpose(back, (2, 0, 1, 3))
    return (analysis, factor, mean_weights.reshape(MEMBERS))


def solution(mesh):
    placed = (
        P("ens", None, "map", None),
        P(),
        P(),
        P(),
        P(),
        P("map"),
        P("map"),
        P("map"),
        P("map"),
    )
    return jax.shard_map(
        on_device,
        mesh=mesh,
        in_specs=placed,
        out_specs=(P("ens", None, "map", None), P(), P()),
        check_vma=False,
    )
```

```python
import functools
import math

import jax
import jax.numpy as jnp
from jax import lax
from jax.experimental import pallas as pl
from jax.experimental.pallas import tpu as pltpu
from jax.sharding import PartitionSpec as P

FIELDS = 16
HID = 128
ROWS = 4
LON = 1440
RING = 1536
SLOTS = 256
GROUP = 16
PLANES = ROWS * FIELDS
CHUNKS = 2
STEP = 4
N_ENS = 8
MEMBERS = 128
VMEM_LIMIT = 56 * 1024 * 1024


def prepare_kernel(
    tile_ref,
    first_ref,
    bias_in_ref,
    second_ref,
    bias_out_ref,
    index_ref,
    top_ref,
    bottom_ref,
    low_ref,
    middle_ref,
    high_ref,
    bias_ref,
    picks_ref,
    plane_ref,
    *,
    tiles,
):
    tap = lambda ref, row, column: ref[(3 * row + column) * 16 : (3 * row + column + 1) * 16]
    half = bias_in_ref[...] * 0.5
    high = half.astype(jnp.bfloat16).astype(jnp.float32)
    middle = (half - high).astype(jnp.bfloat16).astype(jnp.float32)
    low = half - high - middle
    zeros = jnp.zeros((16, HID), jnp.float32)
    bias = jnp.concatenate([high, middle, low, zeros[:13]], axis=0)
    parts = []
    for r in range(3):
        pieces = []
        for column in range(3):
            for row in range(5):
                known = 0 <= row - r <= 2
                piece = tap(first_ref, row - r, column).astype(jnp.float32) if known else zeros
                pieces.append(piece * 0.5)
        parts.append(jnp.concatenate(pieces + [bias], axis=0).T)
    tile = tile_ref[0]
    inner_top = jnp.where(tile > 0, 1.0, 0.0)
    inner_bottom = jnp.where(tile < tiles - 1, 1.0, 0.0)
    top = jnp.concatenate([parts[0] * inner_top, parts[1], parts[2]], axis=0)
    bottom = jnp.concatenate([parts[0], parts[1], parts[2] * inner_bottom], axis=0)
    top_ref[...] = top.astype(jnp.bfloat16)
    bottom_ref[...] = bottom.astype(jnp.bfloat16)

    rows = 6 * FIELDS
    to = lax.broadcasted_iota(jnp.int32, (rows, rows), 0)
    source = to // 32 * 32 + to % 2 * 16 + to % 32 // 2
    turn = (source == lax.broadcasted_iota(jnp.int32, (rows, rows), 1)).astype(jnp.bfloat16)

    def placed(taps):
        blank = jnp.zeros((16, HID), jnp.bfloat16)
        lines = []
        for column in range(3):
            for line in taps:
                cells = [blank if d is None else tap(second_ref, d, column) for d in line]
                lines.append(jnp.concatenate(cells, axis=1))
        whole = jnp.concatenate(lines, axis=0)
        return jnp.dot(turn, whole, preferred_element_type=jnp.float32).astype(jnp.bfloat16)

    upper = placed(((0, 1), (None, 0)))
    lower = placed(((2, None), (1, 2)))
    low_ref[...] = upper
    middle_ref[...] = jnp.concatenate([lower, upper], axis=0)
    high_ref[...] = lower

    group = 16 * FIELDS
    field = lax.broadcasted_iota(jnp.int32, (group, FIELDS), 0) // 16
    mine = field == lax.broadcasted_iota(jnp.int32, (group, FIELDS), 1)
    bias_ref[...] = jnp.sum(jnp.where(mine, bias_out_ref[...], 0.0), axis=1, keepdims=True)

    entry = index_ref[...]
    bound = (lax.broadcasted_iota(jnp.int32, (PLANES, SLOTS), 0) + 1) * LON
    plane = jnp.sum(jnp.where(entry >= bound, 1, 0), axis=0, keepdims=True)
    plane_ref[...] = plane
    column = entry - plane * LON
    for at in range(0, RING, 256):
        place = lax.broadcasted_iota(jnp.int32, (256, SLOTS), 0) + at
        picks_ref[at : at + 256, :] = jnp.where(place == column, 1.0, 0.0).astype(jnp.bfloat16)


def prepare(tile, tiles, conv_in, bias_in, conv_out, bias_out, index):
    vmem = pl.BlockSpec(memory_space=pltpu.VMEM)
    shape = jax.ShapeDtypeStruct
    return pl.pallas_call(
        functools.partial(prepare_kernel, tiles=tiles),
        in_specs=[pl.BlockSpec(memory_space=pltpu.SMEM)] + [vmem] * 5,
        out_specs=[vmem] * 8,
        out_shape=[
            shape((3 * HID, 256), jnp.bfloat16),
            shape((3 * HID, 256), jnp.bfloat16),
            shape((6 * FIELDS, 2 * HID), jnp.bfloat16),
            shape((12 * FIELDS, 2 * HID), jnp.bfloat16),
            shape((6 * FIELDS, 2 * HID), jnp.bfloat16),
            shape((16 * FIELDS, 1), jnp.float32),
            shape((RING, SLOTS), jnp.bfloat16),
            shape((1, SLOTS), jnp.int32),
        ],
        cost_estimate=cost(3),
    )(
        tile.astype(jnp.int32).reshape(1),
        jnp.transpose(conv_in, (2, 3, 1, 0)).reshape(9 * FIELDS, HID),
        bias_in.reshape(1, HID),
        jnp.transpose(conv_out, (2, 3, 0, 1)).reshape(9 * FIELDS, HID),
        bias_out.reshape(1, FIELDS),
        index.reshape(1, SLOTS),
    )


def forecast_kernel(
    x_ref,
    base_ref,
    top_ref,
    bottom_ref,
    first_top_ref,
    first_bottom_ref,
    low_ref,
    middle_ref,
    high_ref,
    bias_ref,
    picks_ref,
    plane_ref,
    earlier_ref,
    fields_ref,
    observed_ref,
    held_ref,
):
    step = pl.program_id(0)
    ones = jnp.ones((16, RING), jnp.bfloat16)
    part = PLANES // 2

    def changes(member):
        stack = jnp.concatenate(
            [
                top_ref[member].reshape(2 * FIELDS, LON),
                x_ref[member].reshape(PLANES, LON),
                bottom_ref[member].reshape(2 * FIELDS, LON),
            ],
            axis=0,
        )
        ring = jnp.concatenate([stack, stack[:, :64], stack[:, LON - 32 :]], axis=1)
        left = pltpu.roll(ring, 1, 1)
        right = pltpu.roll(ring, RING - 1, 1)

        def hidden_rows(at, weights_ref):
            to = at + 5 * FIELDS
            taps = jnp.concatenate([left[at:to], ring[at:to], right[at:to], ones], axis=0)
            half = jnp.dot(weights_ref[...], taps, preferred_element_type=jnp.float32)
            return (half * jnp.tanh(half) + half).astype(jnp.bfloat16)

        hidden = jnp.concatenate(
            [hidden_rows(0, first_top_ref), hidden_rows(3 * FIELDS, first_bottom_ref)], axis=0
        )

        def outer(weights_ref, pair):
            rows = hidden[2 * HID * pair : 2 * HID * (pair + 1)]
            return jnp.dot(weights_ref[...], rows, preferred_element_type=jnp.float32)

        both = outer(middle_ref, 1)
        for taps in (both[: 3 * part] + outer(low_ref, 0), both[3 * part :] + outer(high_ref, 2)):
            yield (
                pltpu.roll(taps[:part], 1, 1)
                + taps[part : 2 * part]
                + pltpu.roll(taps[2 * part :], RING - 1, 1)
            )

    sub = lax.broadcasted_iota(jnp.int32, (8, RING), 0)
    members = [list(changes(member)) for member in range(STEP)]
    for field in range(FIELDS):
        at, by = field // 4 * 8, field % 4 * 2
        halves = []
        for pair in range(2):
            moved = []
            for k, parts in enumerate(members):
                rows = parts[pair][at : at + 8]
                turn = (2 * k - by) % 8
                moved.append(pltpu.roll(rows, turn, 0) if turn else rows)
            first = jnp.where(sub < 2, moved[0], moved[1])
            last = jnp.where(sub < 6, moved[2], moved[3])
            halves.append(jnp.where(sub < 4, first, last))
        low, high = field * 16, field * 16 + 16
        base = base_ref[0, low:high, :].astype(jnp.float32) + bias_ref[low:high, :]
        base = jnp.concatenate([base, base[:, : RING - LON]], axis=1)
        a, b = base[:8], base[8:]
        a4, a6 = pltpu.roll(a, 4, 0), pltpu.roll(a, 6, 0)
        b2, b4 = pltpu.roll(b, 2, 0), pltpu.roll(b, 4, 0)
        choose = lambda *four: jnp.where(
            sub < 4, jnp.where(sub < 2, *four[:2]), jnp.where(sub < 6, *four[2:])
        )
        base = jnp.concatenate([choose(a, a6, b4, b2), choose(a6, a4, b2, b)], axis=0)
        own = (base + jnp.concatenate(halves, axis=0)).astype(jnp.bfloat16)
        for pair in range(2):
            block = own[8 * pair : 8 * pair + 8, :LON]
            fields_ref[field // 2, field % 2 * 2 + pair, 0] = block
        held_ref[pl.ds(pl.multiple_of(step * 16 * FIELDS + low, 16), 16), :] = own

    @pl.when(step == pl.num_programs(0) - 1)
    def _():
        rows = held_ref.shape[0]
        picked = jnp.dot(held_ref[...], picks_ref[...], preferred_element_type=jnp.float32)
        row = lax.broadcasted_iota(jnp.int32, (rows, SLOTS), 0)
        here = row % 256 // 8 * 2 + row % 2 == plane_ref[...]
        found = jnp.where(here, picked, 0.0).astype(jnp.bfloat16)
        count = rows // PLANES
        column = lax.broadcasted_iota(jnp.int32, (count, rows), 1)
        member = column // 256 * STEP + column % 8 // 2
        mine = member == lax.broadcasted_iota(jnp.int32, (count, rows), 0)
        seen = jnp.dot(
            mine.astype(jnp.bfloat16), found, preferred_element_type=jnp.float32
        )
        if earlier_ref is not None:
            seen = jnp.concatenate([earlier_ref[...], seen], axis=0)
        observed_ref[...] = seen


def cost(microseconds):
    return pl.CostEstimate(
        flops=int(microseconds * 1e9), transcendentals=0, bytes_accessed=int(microseconds * 1e6)
    )


def forecast(start, own, base, top, bottom, shared, earlier):
    count = top.shape[0]
    steps = count // STEP
    first = start // STEP
    whole = lambda array: pl.BlockSpec(array.shape, lambda m: (0,) * array.ndim)
    kernel = forecast_kernel
    if earlier is None:
        kernel = lambda *refs: forecast_kernel(*refs[:-3], None, *refs[-3:])
        seen = count
    else:
        shared = [*shared, earlier]
        seen = count + earlier.shape[0]
    return pl.pallas_call(
        kernel,
        grid=(steps,),
        in_specs=[
            pl.BlockSpec((STEP, ROWS, FIELDS, LON), lambda m: (first + m, 0, 0, 0)),
            pl.BlockSpec((1, 16 * FIELDS, LON), lambda m: (first + m, 0, 0)),
            pl.BlockSpec((STEP, 2, FIELDS, LON), lambda m: (m, 0, 0, 0)),
            pl.BlockSpec((STEP, 2, FIELDS, LON), lambda m: (m, 0, 0, 0)),
        ]
        + [whole(array) for array in shared],
        out_specs=[
            pl.BlockSpec((N_ENS, 4, 1, 8, LON), lambda m: (0, 0, m, 0, 0)),
            pl.BlockSpec((seen, SLOTS), lambda m: (0, 0)),
        ],
        out_shape=[
            jax.ShapeDtypeStruct((N_ENS, 4, steps, 8, LON), jnp.bfloat16),
            jax.ShapeDtypeStruct((seen, SLOTS), jnp.float32),
        ],
        scratch_shapes=[pltpu.VMEM((count * PLANES, RING), jnp.bfloat16)],
        cost_estimate=cost(2 * count),
        compiler_params=pltpu.CompilerParams(vmem_limit_bytes=VMEM_LIMIT),
    )(own, base, top, bottom, *shared)


def products_kernel(place_ref, count_ref, value_ref, sigma_ref, *refs):
    pieces, out_ref, held_ref = refs[: N_ENS // 2], refs[N_ENS // 2], refs[N_ENS // 2 + 1]
    for step in range(N_ENS):
        at = pl.multiple_of((place_ref[0] ^ step) * GROUP, GROUP)
        low = step % 2 * GROUP
        held_ref[pl.ds(at, GROUP), :] = pieces[step // 2][low : low + GROUP, :]
    observed = held_ref[...]
    mean = jnp.sum(observed, axis=0, keepdims=True) / MEMBERS
    slot = lax.broadcasted_iota(jnp.int32, (1, SLOTS), 1)
    live = (slot < count_ref[0]).astype(jnp.float32)
    sigma = sigma_ref[...]
    anomalies = (observed - mean) * (live / (sigma * math.sqrt(MEMBERS - 1)))
    innov = live * (value_ref[...] - mean) / sigma
    left = jnp.concatenate([anomalies, jnp.broadcast_to(innov, (8, SLOTS))], axis=0)
    out_ref[...] = lax.dot_general(
        left,
        anomalies,
        (((1,), (1,)), ((), ())),
        precision=lax.Precision.HIGHEST,
        preferred_element_type=jnp.float32,
    )


def products(pieces, places, count, value, sigma):
    vmem = pl.BlockSpec(memory_space=pltpu.VMEM)
    smem = pl.BlockSpec(memory_space=pltpu.SMEM)
    return pl.pallas_call(
        products_kernel,
        in_specs=[smem, smem] + [vmem] * (2 + N_ENS // 2),
        out_specs=vmem,
        out_shape=jax.ShapeDtypeStruct((MEMBERS + 8, MEMBERS), jnp.float32),
        cost_estimate=cost(1),
        scratch_shapes=[pltpu.VMEM((MEMBERS, SLOTS), jnp.float32)],
    )(places, count, value.reshape(1, SLOTS), sigma.reshape(1, SLOTS), *pieces)


def transform_kernel(a_ref, b_ref, c_ref, d_ref, factor_ref, weights_ref, transform_ref):
    n = MEMBERS
    total = (a_ref[...] + b_ref[...]) + (c_ref[...] + d_ref[...])
    row = lax.broadcasted_iota(jnp.int32, (n, n), 0)
    column = lax.broadcasted_iota(jnp.int32, (n, n), 1)
    eye = (row == column).astype(jnp.float32)
    gram = total[0:n] + eye
    blocks = [[gram[b : b + 8], eye[b : b + 8]] for b in range(0, n, 8)]
    within = lax.broadcasted_iota(jnp.int32, (8, n), 0)
    wide = lambda value: jnp.broadcast_to(value, (8, n))
    for b in range(n // 8):
        upper, inverse = blocks[b]
        columns = [wide(upper[:, 8 * b + k : 8 * b + k + 1]) for k in range(8)]
        scales, steps, rows = [], [], []
        for k in range(8):
            scale = lax.rsqrt(wide(columns[k][k : k + 1]))
            share = columns[k] * scale
            step = {}
            for later in range(k + 1, 8):
                step[later] = wide(share[later : later + 1])
                columns[later] = columns[later] - share * step[later]
            upper_row = wide(upper[k : k + 1]) * scale
            inverse_row = wide(inverse[k : k + 1]) * scale
            share = jnp.where(within > k, share, 0.0)
            upper = jnp.where(within == k, upper_row, upper - share * upper_row)
            inverse = jnp.where(within == k, inverse_row, inverse - share * inverse_row)
            scales.append(scale)
            steps.append(step)
            rows.append((upper_row, inverse_row))
        for t in range(b + 1, n // 8):
            later_upper, later_inverse = blocks[t]
            columns = [wide(later_upper[:, 8 * b + k : 8 * b + k + 1]) for k in range(8)]
            for k in range(8):
                share = columns[k] * scales[k]
                for later in range(k + 1, 8):
                    columns[later] = columns[later] - share * steps[k][later]
                later_upper = later_upper - share * rows[k][0]
                later_inverse = later_inverse - share * rows[k][1]
            blocks[t] = [later_upper, later_inverse]
        blocks[b] = [upper, inverse]
    upper = jnp.concatenate([pair[0] for pair in blocks], axis=0)
    inverse = jnp.concatenate([pair[1] for pair in blocks], axis=0)
    factor_ref[...] = jnp.where(row <= column, upper, 0.0).T
    proj = total[n : n + 1]
    middle = jnp.sum(inverse * proj, axis=1, keepdims=True)
    weights = jnp.sum(inverse * middle, axis=0, keepdims=True) / math.sqrt(n - 1)
    weights_ref[...] = weights
    coeff = inverse + weights
    transform = coeff - jnp.mean(coeff, axis=1, keepdims=True) + 1.0 / n
    transform_ref[...] = transform.astype(jnp.bfloat16)


def transform_of(parts):
    vmem = pl.BlockSpec(memory_space=pltpu.VMEM)
    return pl.pallas_call(
        transform_kernel,
        in_specs=[vmem] * 4,
        out_specs=[vmem, vmem, vmem],
        out_shape=[
            jax.ShapeDtypeStruct((MEMBERS, MEMBERS), jnp.float32),
            jax.ShapeDtypeStruct((1, MEMBERS), jnp.float32),
            jax.ShapeDtypeStruct((MEMBERS, MEMBERS), jnp.bfloat16),
        ],
        cost_estimate=cost(1),
        compiler_params=pltpu.CompilerParams(vmem_limit_bytes=60 * 1024 * 1024),
    )(*parts)


def update_kernel(transform_ref, early_ref, late_ref, out_ref, spread_ref):
    rows = MEMBERS * 2
    half = rows // 2

    @pl.when(pl.program_id(0) == 0)
    def _():
        shape = (rows, MEMBERS)
        row = lax.broadcasted_iota(jnp.int32, shape, 0)
        column = lax.broadcasted_iota(jnp.int32, shape, 1)
        held = row % half // 16 * GROUP + row // half * 8 + row % 16 // 2
        wanted = row // 32 * GROUP + row % GROUP
        repeat = (wanted == column).astype(jnp.bfloat16)
        placed = (held == column).astype(jnp.bfloat16)
        tall = jnp.dot(repeat, transform_ref[...], preferred_element_type=jnp.float32)
        wide = lax.dot_general(
            tall.astype(jnp.bfloat16),
            placed,
            (((1,), (1,)), ((), ())),
            preferred_element_type=jnp.float32,
        )
        own = lax.broadcasted_iota(jnp.int32, (rows, rows), 0) // GROUP % 2
        same = own == lax.broadcasted_iota(jnp.int32, (rows, rows), 1) % 2
        spread_ref[...] = jnp.where(same, wide, 0.0).astype(jnp.bfloat16)

    fields = jnp.concatenate(
        [early_ref[:, 0].reshape(half, LON), late_ref[:, 0].reshape(half, LON)], axis=0
    )
    mixed = jnp.dot(spread_ref[...], fields, preferred_element_type=jnp.float32)
    out_ref[:, 0] = mixed.astype(jnp.bfloat16).reshape(N_ENS, GROUP * 2, LON)


def update(transform, early, late):
    rows = MEMBERS * 2
    half = pl.BlockSpec((N_ENS, 1, 16, LON), lambda q: (0, q, 0, 0))
    joined = (N_ENS, 4, 16, LON)
    return pl.pallas_call(
        update_kernel,
        grid=(4,),
        in_specs=[pl.BlockSpec((MEMBERS, MEMBERS), lambda q: (0, 0)), half, half],
        out_specs=pl.BlockSpec((N_ENS, 1, GROUP * 2, LON), lambda q: (0, q, 0, 0)),
        out_shape=jax.ShapeDtypeStruct((N_ENS, 4, GROUP * 2, LON), jnp.bfloat16),
        scratch_shapes=[pltpu.VMEM((rows, rows), jnp.bfloat16)],
        cost_estimate=cost(3),
        compiler_params=pltpu.CompilerParams(vmem_limit_bytes=VMEM_LIMIT),
    )(transform, early.reshape(joined), late.reshape(joined))


def on_device(
    ensemble_weather,
    conv_in,
    bias_in,
    conv_out,
    bias_out,
    observed_entry_index,
    obs_count,
    obs_value,
    obs_sigma,
):
    tiles = lax.axis_size("map")
    tile = lax.axis_index("map")
    own_place = lax.axis_index("ens")
    down = [(i, i + 1) for i in range(tiles - 1)]
    up = [(i + 1, i) for i in range(tiles - 1)]

    def swap(value, axis, step):
        pairs = [(i, i ^ step) for i in range(lax.axis_size(axis))]
        return lax.ppermute(value, axis, pairs)

    share = GROUP // CHUNKS
    exchange = lambda value: lax.all_to_all(
        value, "ens", split_axis=0, concat_axis=0, tiled=True
    )
    own = jnp.transpose(ensemble_weather, (0, 2, 1, 3))

    def edges(chunk):
        part = own[chunk * share : (chunk + 1) * share]
        return part[:, ROWS - 2 :], part[:, :2]

    def halo(rows):
        return lax.ppermute(rows[0], "map", down), lax.ppermute(rows[1], "map", up)

    halos = [halo(edges(0))]
    shared = prepare(
        tile, tiles, conv_in, bias_in, conv_out, bias_out, observed_entry_index
    )
    base = jnp.transpose(
        ensemble_weather.reshape(GROUP // STEP, STEP, FIELDS, ROWS, LON), (0, 2, 1, 3, 4)
    ).reshape(GROUP // STEP, STEP * PLANES, LON)
    next_edges, shared, base = lax.optimization_barrier((edges(1), shared, base))
    halos.append(halo(next_edges))
    fields, observed = [], None
    for chunk, (top, bottom) in enumerate(halos):
        moved, observed = forecast(chunk * share, own, base, top, bottom, shared, observed)
        fields.append(moved)
    early = exchange(fields[0])
    observed = jnp.concatenate([observed, swap(observed, "ens", 1)], axis=0)
    pieces = [observed] + [swap(observed, "ens", step) for step in range(2, N_ENS, 2)]
    places = own_place.astype(jnp.int32).reshape(1)
    pieces, late, early = lax.optimization_barrier((pieces, fields[1], early))
    late = exchange(late)
    part = products(pieces, places, obs_count, obs_value, obs_sigma)
    near = [part] + [swap(part, "map", step) for step in (1, 2, 3)]
    row = (near[0] + near[1]) + (near[2] + near[3])
    factor, mean_weights, transform = transform_of(
        [row] + [swap(row, "map", step) for step in (4, 8, 12)]
    )
    back = exchange(update(transform, early, late))
    back = back.reshape(FIELDS, ROWS, GROUP, LON)
    analysis = jnp.transpose(back, (2, 0, 1, 3))
    return (analysis, factor, mean_weights.reshape(MEMBERS))


def solution(mesh):
    placed = (
        P("ens", None, "map", None),
        P(),
        P(),
        P(),
        P(),
        P("map"),
        P("map"),
        P("map"),
        P("map"),
    )
    return jax.shard_map(
        on_device,
        mesh=mesh,
        in_specs=placed,
        out_specs=(P("ens", None, "map", None), P(), P()),
        check_vma=False,
    )
```

```python
import functools
import math

import jax
import jax.numpy as jnp
from jax import lax
from jax.experimental import pallas as pl
from jax.experimental.pallas import tpu as pltpu
from jax.sharding import PartitionSpec as P

FIELDS = 16
HID = 128
ROWS = 4
LON = 1440
RING = 1536
SLOTS = 256
GROUP = 16
PLANES = ROWS * FIELDS
CHUNKS = 2
STEP = 4
N_ENS = 8
MEMBERS = 128
VMEM_LIMIT = 56 * 1024 * 1024


def prepare_kernel(
    tile_ref,
    first_ref,
    bias_in_ref,
    second_ref,
    bias_out_ref,
    index_ref,
    top_ref,
    bottom_ref,
    low_ref,
    middle_ref,
    high_ref,
    bias_ref,
    picks_ref,
    plane_ref,
    *,
    tiles,
):
    tap = lambda ref, row, column: ref[(3 * row + column) * 16 : (3 * row + column + 1) * 16]
    half = bias_in_ref[...] * 0.5
    high = half.astype(jnp.bfloat16).astype(jnp.float32)
    middle = (half - high).astype(jnp.bfloat16).astype(jnp.float32)
    low = half - high - middle
    zeros = jnp.zeros((16, HID), jnp.float32)
    bias = jnp.concatenate([high, middle, low, zeros[:13]], axis=0)
    parts = []
    for r in range(3):
        pieces = []
        for column in range(3):
            for row in range(5):
                known = 0 <= row - r <= 2
                piece = tap(first_ref, row - r, column).astype(jnp.float32) if known else zeros
                pieces.append(piece * 0.5)
        parts.append(jnp.concatenate(pieces + [bias], axis=0).T)
    tile = tile_ref[0]
    inner_top = jnp.where(tile > 0, 1.0, 0.0)
    inner_bottom = jnp.where(tile < tiles - 1, 1.0, 0.0)
    top = jnp.concatenate([parts[0] * inner_top, parts[1], parts[2]], axis=0)
    bottom = jnp.concatenate([parts[0], parts[1], parts[2] * inner_bottom], axis=0)
    top_ref[...] = top.astype(jnp.bfloat16)
    bottom_ref[...] = bottom.astype(jnp.bfloat16)

    rows = 6 * FIELDS
    to = lax.broadcasted_iota(jnp.int32, (rows, rows), 0)
    source = to // 32 * 32 + to % 2 * 16 + to % 32 // 2
    turn = (source == lax.broadcasted_iota(jnp.int32, (rows, rows), 1)).astype(jnp.bfloat16)

    def placed(taps):
        blank = jnp.zeros((16, HID), jnp.bfloat16)
        lines = []
        for column in range(3):
            for line in taps:
                cells = [blank if d is None else tap(second_ref, d, column) for d in line]
                lines.append(jnp.concatenate(cells, axis=1))
        whole = jnp.concatenate(lines, axis=0)
        return jnp.dot(turn, whole, preferred_element_type=jnp.float32).astype(jnp.bfloat16)

    upper = placed(((0, 1), (None, 0)))
    lower = placed(((2, None), (1, 2)))
    low_ref[...] = upper
    middle_ref[...] = jnp.concatenate([lower, upper], axis=0)
    high_ref[...] = lower

    group = 16 * FIELDS
    field = lax.broadcasted_iota(jnp.int32, (group, FIELDS), 0) // 16
    mine = field == lax.broadcasted_iota(jnp.int32, (group, FIELDS), 1)
    bias_ref[...] = jnp.sum(jnp.where(mine, bias_out_ref[...], 0.0), axis=1, keepdims=True)

    entry = index_ref[...]
    bound = (lax.broadcasted_iota(jnp.int32, (PLANES, SLOTS), 0) + 1) * LON
    plane = jnp.sum(jnp.where(entry >= bound, 1, 0), axis=0, keepdims=True)
    plane_ref[...] = plane
    column = entry - plane * LON
    for at in range(0, RING, 256):
        place = lax.broadcasted_iota(jnp.int32, (256, SLOTS), 0) + at
        picks_ref[at : at + 256, :] = jnp.where(place == column, 1.0, 0.0).astype(jnp.bfloat16)


def prepare(tile, tiles, conv_in, bias_in, conv_out, bias_out, index):
    vmem = pl.BlockSpec(memory_space=pltpu.VMEM)
    shape = jax.ShapeDtypeStruct
    return pl.pallas_call(
        functools.partial(prepare_kernel, tiles=tiles),
        in_specs=[pl.BlockSpec(memory_space=pltpu.SMEM)] + [vmem] * 5,
        out_specs=[vmem] * 8,
        out_shape=[
            shape((3 * HID, 256), jnp.bfloat16),
            shape((3 * HID, 256), jnp.bfloat16),
            shape((6 * FIELDS, 2 * HID), jnp.bfloat16),
            shape((12 * FIELDS, 2 * HID), jnp.bfloat16),
            shape((6 * FIELDS, 2 * HID), jnp.bfloat16),
            shape((16 * FIELDS, 1), jnp.float32),
            shape((RING, SLOTS), jnp.bfloat16),
            shape((1, SLOTS), jnp.int32),
        ],
        cost_estimate=cost(3),
    )(
        tile.astype(jnp.int32).reshape(1),
        jnp.transpose(conv_in, (2, 3, 1, 0)).reshape(9 * FIELDS, HID),
        bias_in.reshape(1, HID),
        jnp.transpose(conv_out, (2, 3, 0, 1)).reshape(9 * FIELDS, HID),
        bias_out.reshape(1, FIELDS),
        index.reshape(1, SLOTS),
    )


def forecast_kernel(
    x_ref,
    base_ref,
    top_ref,
    bottom_ref,
    first_top_ref,
    first_bottom_ref,
    low_ref,
    middle_ref,
    high_ref,
    bias_ref,
    picks_ref,
    plane_ref,
    earlier_ref,
    fields_ref,
    observed_ref,
    held_ref,
):
    step = pl.program_id(0)
    ones = jnp.ones((16, RING), jnp.bfloat16)
    part = PLANES // 2

    def changes(member):
        stack = jnp.concatenate(
            [
                top_ref[member].reshape(2 * FIELDS, LON),
                x_ref[member].reshape(PLANES, LON),
                bottom_ref[member].reshape(2 * FIELDS, LON),
            ],
            axis=0,
        )
        ring = jnp.concatenate([stack, stack[:, :64], stack[:, LON - 32 :]], axis=1)
        left = pltpu.roll(ring, 1, 1)
        right = pltpu.roll(ring, RING - 1, 1)

        def hidden_rows(at, weights_ref):
            to = at + 5 * FIELDS
            taps = jnp.concatenate([left[at:to], ring[at:to], right[at:to], ones], axis=0)
            half = jnp.dot(weights_ref[...], taps, preferred_element_type=jnp.float32)
            return (half * jnp.tanh(half) + half).astype(jnp.bfloat16)

        hidden = jnp.concatenate(
            [hidden_rows(0, first_top_ref), hidden_rows(3 * FIELDS, first_bottom_ref)], axis=0
        )

        def outer(weights_ref, pair):
            rows = hidden[2 * HID * pair : 2 * HID * (pair + 1)]
            return jnp.dot(weights_ref[...], rows, preferred_element_type=jnp.float32)

        both = outer(middle_ref, 1)
        for taps in (both[: 3 * part] + outer(low_ref, 0), both[3 * part :] + outer(high_ref, 2)):
            yield (
                pltpu.roll(taps[:part], 1, 1)
                + taps[part : 2 * part]
                + pltpu.roll(taps[2 * part :], RING - 1, 1)
            )

    sub = lax.broadcasted_iota(jnp.int32, (8, RING), 0)
    pairs = []
    for pair in range(STEP // 2):
        sources = [*changes(2 * pair), *changes(2 * pair + 1)]
        blocks = []
        for field in range(FIELDS):
            at, by = field // 4 * 8, field % 4 * 2
            moved = [
                pltpu.roll(source[at : at + 8], (2 * k - by) % 8, 0) if (2 * k - by) % 8 else source[at : at + 8]
                for k, source in enumerate(sources)
            ]
            first = jnp.where(sub < 2, moved[0], moved[1])
            last = jnp.where(sub < 6, moved[2], moved[3])
            blocks.append(jnp.where(sub < 4, first, last))
        pairs.append(blocks)
    for field in range(FIELDS):
        low, high = field * 16, field * 16 + 16
        base = base_ref[0, low:high, :].astype(jnp.float32) + bias_ref[low:high, :]
        base = jnp.concatenate([base, base[:, : RING - LON]], axis=1)
        change = jnp.concatenate([blocks[field] for blocks in pairs], axis=0)
        own = (base + change).astype(jnp.bfloat16)
        fields_ref[field // 2, field % 2] = own[:, :LON]
        held_ref[pl.ds(pl.multiple_of(step * 16 * FIELDS + low, 16), 16), :] = own

    @pl.when(step == pl.num_programs(0) - 1)
    def _():
        rows = held_ref.shape[0]
        picked = jnp.dot(held_ref[...], picks_ref[...], preferred_element_type=jnp.float32)
        row = lax.broadcasted_iota(jnp.int32, (rows, SLOTS), 0)
        here = row % 256 // 16 * ROWS + row % ROWS == plane_ref[...]
        found = jnp.where(here, picked, 0.0).astype(jnp.bfloat16)
        count = rows // PLANES
        column = lax.broadcasted_iota(jnp.int32, (count, rows), 1)
        member = column // 256 * STEP + column % 16 // ROWS
        mine = member == lax.broadcasted_iota(jnp.int32, (count, rows), 0)
        seen = jnp.dot(
            mine.astype(jnp.bfloat16), found, preferred_element_type=jnp.float32
        )
        if earlier_ref is not None:
            seen = jnp.concatenate([earlier_ref[...], seen], axis=0)
        observed_ref[...] = seen


def cost(microseconds):
    return pl.CostEstimate(
        flops=int(microseconds * 1e9), transcendentals=0, bytes_accessed=int(microseconds * 1e6)
    )


def forecast(start, own, base, top, bottom, shared, earlier):
    count = top.shape[0]
    steps = count // STEP
    first = start // STEP
    whole = lambda array: pl.BlockSpec(array.shape, lambda m: (0,) * array.ndim)
    kernel = forecast_kernel
    if earlier is None:
        kernel = lambda *refs: forecast_kernel(*refs[:-3], None, *refs[-3:])
        seen = count
    else:
        shared = [*shared, earlier]
        seen = count + earlier.shape[0]
    return pl.pallas_call(
        kernel,
        grid=(steps,),
        in_specs=[
            pl.BlockSpec((STEP, ROWS, FIELDS, LON), lambda m: (first + m, 0, 0, 0)),
            pl.BlockSpec((1, 16 * FIELDS, LON), lambda m: (first + m, 0, 0)),
            pl.BlockSpec((STEP, 2, FIELDS, LON), lambda m: (m, 0, 0, 0)),
            pl.BlockSpec((STEP, 2, FIELDS, LON), lambda m: (m, 0, 0, 0)),
        ]
        + [whole(array) for array in shared],
        out_specs=[
            pl.BlockSpec((N_ENS, 2, 16, LON), lambda m: (0, 0, m, 0)),
            pl.BlockSpec((seen, SLOTS), lambda m: (0, 0)),
        ],
        out_shape=[
            jax.ShapeDtypeStruct((N_ENS, 2, count * ROWS, LON), jnp.bfloat16),
            jax.ShapeDtypeStruct((seen, SLOTS), jnp.float32),
        ],
        scratch_shapes=[pltpu.VMEM((count * PLANES, RING), jnp.bfloat16)],
        cost_estimate=cost(2 * count),
        compiler_params=pltpu.CompilerParams(vmem_limit_bytes=VMEM_LIMIT),
    )(own, base, top, bottom, *shared)


def products_kernel(place_ref, count_ref, value_ref, sigma_ref, *refs):
    pieces, out_ref, held_ref = refs[: N_ENS // 2], refs[N_ENS // 2], refs[N_ENS // 2 + 1]
    for step in range(N_ENS):
        at = pl.multiple_of((place_ref[0] ^ step) * GROUP, GROUP)
        low = step % 2 * GROUP
        held_ref[pl.ds(at, GROUP), :] = pieces[step // 2][low : low + GROUP, :]
    observed = held_ref[...]
    mean = jnp.sum(observed, axis=0, keepdims=True) / MEMBERS
    slot = lax.broadcasted_iota(jnp.int32, (1, SLOTS), 1)
    live = (slot < count_ref[0]).astype(jnp.float32)
    sigma = sigma_ref[...]
    anomalies = (observed - mean) * (live / (sigma * math.sqrt(MEMBERS - 1)))
    innov = live * (value_ref[...] - mean) / sigma
    left = jnp.concatenate([anomalies, jnp.broadcast_to(innov, (8, SLOTS))], axis=0)
    out_ref[...] = lax.dot_general(
        left,
        anomalies,
        (((1,), (1,)), ((), ())),
        precision=lax.Precision.HIGHEST,
        preferred_element_type=jnp.float32,
    )


def products(pieces, places, count, value, sigma):
    vmem = pl.BlockSpec(memory_space=pltpu.VMEM)
    smem = pl.BlockSpec(memory_space=pltpu.SMEM)
    return pl.pallas_call(
        products_kernel,
        in_specs=[smem, smem] + [vmem] * (2 + N_ENS // 2),
        out_specs=vmem,
        out_shape=jax.ShapeDtypeStruct((MEMBERS + 8, MEMBERS), jnp.float32),
        cost_estimate=cost(10),
        scratch_shapes=[pltpu.VMEM((MEMBERS, SLOTS), jnp.float32)],
    )(places, count, value.reshape(1, SLOTS), sigma.reshape(1, SLOTS), *pieces)


def transform_kernel(a_ref, b_ref, c_ref, d_ref, factor_ref, weights_ref, transform_ref):
    n = MEMBERS
    total = (a_ref[...] + b_ref[...]) + (c_ref[...] + d_ref[...])
    row = lax.broadcasted_iota(jnp.int32, (n, n), 0)
    column = lax.broadcasted_iota(jnp.int32, (n, n), 1)
    eye = (row == column).astype(jnp.float32)
    gram = total[0:n] + eye
    blocks = [[gram[b : b + 8], eye[b : b + 8]] for b in range(0, n, 8)]
    within = lax.broadcasted_iota(jnp.int32, (8, n), 0)
    wide = lambda value: jnp.broadcast_to(value, (8, n))
    for b in range(n // 8):
        upper, inverse = blocks[b]
        columns = [wide(upper[:, 8 * b + k : 8 * b + k + 1]) for k in range(8)]
        scales, steps, rows = [], [], []
        for k in range(8):
            scale = lax.rsqrt(wide(columns[k][k : k + 1]))
            share = columns[k] * scale
            step = {}
            for later in range(k + 1, 8):
                step[later] = wide(share[later : later + 1])
                columns[later] = columns[later] - share * step[later]
            upper_row = wide(upper[k : k + 1]) * scale
            inverse_row = wide(inverse[k : k + 1]) * scale
            share = jnp.where(within > k, share, 0.0)
            upper = jnp.where(within == k, upper_row, upper - share * upper_row)
            inverse = jnp.where(within == k, inverse_row, inverse - share * inverse_row)
            scales.append(scale)
            steps.append(step)
            rows.append((upper_row, inverse_row))
        for t in range(b + 1, n // 8):
            later_upper, later_inverse = blocks[t]
            columns = [wide(later_upper[:, 8 * b + k : 8 * b + k + 1]) for k in range(8)]
            for k in range(8):
                share = columns[k] * scales[k]
                for later in range(k + 1, 8):
                    columns[later] = columns[later] - share * steps[k][later]
                later_upper = later_upper - share * rows[k][0]
                later_inverse = later_inverse - share * rows[k][1]
            blocks[t] = [later_upper, later_inverse]
        blocks[b] = [upper, inverse]
    upper = jnp.concatenate([pair[0] for pair in blocks], axis=0)
    inverse = jnp.concatenate([pair[1] for pair in blocks], axis=0)
    factor_ref[...] = jnp.where(row <= column, upper, 0.0).T
    proj = total[n : n + 1]
    middle = jnp.sum(inverse * proj, axis=1, keepdims=True)
    weights = jnp.sum(inverse * middle, axis=0, keepdims=True) / math.sqrt(n - 1)
    weights_ref[...] = weights
    coeff = inverse + weights
    transform = coeff - jnp.mean(coeff, axis=1, keepdims=True) + 1.0 / n
    transform_ref[...] = transform.astype(jnp.bfloat16)


def transform_of(parts):
    vmem = pl.BlockSpec(memory_space=pltpu.VMEM)
    return pl.pallas_call(
        transform_kernel,
        in_specs=[vmem] * 4,
        out_specs=[vmem, vmem, vmem],
        out_shape=[
            jax.ShapeDtypeStruct((MEMBERS, MEMBERS), jnp.float32),
            jax.ShapeDtypeStruct((1, MEMBERS), jnp.float32),
            jax.ShapeDtypeStruct((MEMBERS, MEMBERS), jnp.bfloat16),
        ],
        cost_estimate=cost(10),
        compiler_params=pltpu.CompilerParams(vmem_limit_bytes=60 * 1024 * 1024),
    )(*parts)


def update_kernel(transform_ref, early_ref, late_ref, out_ref, spread_ref):
    rows = MEMBERS * ROWS
    half = rows // 2

    @pl.when((pl.program_id(0) == 0) & (pl.program_id(1) == 0))
    def _():
        shape = (rows, MEMBERS)
        row = lax.broadcasted_iota(jnp.int32, shape, 0)
        column = lax.broadcasted_iota(jnp.int32, shape, 1)
        held = row % half // 32 * GROUP + row // half * 8 + row % 32 // ROWS
        wanted = row // 64 * GROUP + row % GROUP
        repeat = (wanted == column).astype(jnp.bfloat16)
        placed = (held == column).astype(jnp.bfloat16)
        tall = jnp.dot(repeat, transform_ref[...], preferred_element_type=jnp.float32)
        wide = lax.dot_general(
            tall.astype(jnp.bfloat16),
            placed,
            (((1,), (1,)), ((), ())),
            preferred_element_type=jnp.float32,
        )
        own = lax.broadcasted_iota(jnp.int32, (rows, rows), 0) // GROUP % ROWS
        same = own == lax.broadcasted_iota(jnp.int32, (rows, rows), 1) % ROWS
        spread_ref[...] = jnp.where(same, wide, 0.0).astype(jnp.bfloat16)

    width = early_ref.shape[-1]
    fields = jnp.concatenate(
        [early_ref[:, 0].reshape(half, width), late_ref[:, 0].reshape(half, width)], axis=0
    )
    mixed = jnp.dot(spread_ref[...], fields, preferred_element_type=jnp.float32)
    out_ref[:, 0] = mixed.astype(jnp.bfloat16).reshape(N_ENS, GROUP * ROWS, width)


def update(transform, early, late):
    rows = MEMBERS * ROWS
    half = pl.BlockSpec((N_ENS, 1, 8 * ROWS, RING // 2), lambda c, x: (0, c, 0, x))
    return pl.pallas_call(
        update_kernel,
        grid=(2, 2),
        in_specs=[pl.BlockSpec((MEMBERS, MEMBERS), lambda c, x: (0, 0)), half, half],
        out_specs=pl.BlockSpec(
            (N_ENS, 1, GROUP * ROWS, RING // 2), lambda c, x: (0, c, 0, x)
        ),
        out_shape=jax.ShapeDtypeStruct((N_ENS, 2, GROUP * ROWS, LON), jnp.bfloat16),
        scratch_shapes=[pltpu.VMEM((rows, rows), jnp.bfloat16)],
        cost_estimate=cost(4),
        compiler_params=pltpu.CompilerParams(vmem_limit_bytes=VMEM_LIMIT),
    )(transform, early, late)


def on_device(
    ensemble_weather,
    conv_in,
    bias_in,
    conv_out,
    bias_out,
    observed_entry_index,
    obs_count,
    obs_value,
    obs_sigma,
):
    tiles = lax.axis_size("map")
    tile = lax.axis_index("map")
    own_place = lax.axis_index("ens")
    down = [(i, i + 1) for i in range(tiles - 1)]
    up = [(i + 1, i) for i in range(tiles - 1)]

    def swap(value, axis, step):
        pairs = [(i, i ^ step) for i in range(lax.axis_size(axis))]
        return lax.ppermute(value, axis, pairs)

    share = GROUP // CHUNKS
    exchange = lambda value: lax.all_to_all(
        value, "ens", split_axis=0, concat_axis=0, tiled=True
    )
    own = jnp.transpose(ensemble_weather, (0, 2, 1, 3))

    def edges(chunk):
        part = own[chunk * share : (chunk + 1) * share]
        return part[:, ROWS - 2 :], part[:, :2]

    def halo(rows):
        return lax.ppermute(rows[0], "map", down), lax.ppermute(rows[1], "map", up)

    halos = [halo(edges(0))]
    shared = prepare(
        tile, tiles, conv_in, bias_in, conv_out, bias_out, observed_entry_index
    )
    base = jnp.transpose(
        ensemble_weather.reshape(GROUP // STEP, STEP, FIELDS, ROWS, LON), (0, 2, 1, 3, 4)
    ).reshape(GROUP // STEP, STEP * PLANES, LON)
    next_edges, shared, base = lax.optimization_barrier((edges(1), shared, base))
    halos.append(halo(next_edges))
    fields, observed = [], None
    for chunk, (top, bottom) in enumerate(halos):
        moved, observed = forecast(chunk * share, own, base, top, bottom, shared, observed)
        fields.append(moved)
    early = exchange(fields[0])
    observed = jnp.concatenate([observed, swap(observed, "ens", 1)], axis=0)
    pieces = [observed] + [swap(observed, "ens", step) for step in range(2, N_ENS, 2)]
    places = own_place.astype(jnp.int32).reshape(1)
    pieces, late, early = lax.optimization_barrier((pieces, fields[1], early))
    late = exchange(late)
    part = products(pieces, places, obs_count, obs_value, obs_sigma)
    near = [part] + [swap(part, "map", step) for step in (1, 2, 3)]
    row = (near[0] + near[1]) + (near[2] + near[3])
    factor, mean_weights, transform = transform_of(
        [row] + [swap(row, "map", step) for step in (4, 8, 12)]
    )
    back = exchange(update(transform, early, late))
    back = back.reshape(FIELDS, ROWS, GROUP, LON)
    analysis = jnp.transpose(back, (2, 0, 1, 3))
    return (analysis, factor, mean_weights.reshape(MEMBERS))


def solution(mesh):
    placed = (
        P("ens", None, "map", None),
        P(),
        P(),
        P(),
        P(),
        P("map"),
        P("map"),
        P("map"),
        P("map"),
    )
    return jax.shard_map(
        on_device,
        mesh=mesh,
        in_specs=placed,
        out_specs=(P("ens", None, "map", None), P(), P()),
        check_vma=False,
    )
```
